32 devices in a mesh: ctx: 8 (over z, y), ulysses: 4 (over x, core).
Axes of the slice: x: 2, y: 2, z: 4, core: 2. Of those that a mesh axis runs over, the one named last changes fastest.
Arguments:
- queries: bfloat16 [4096, 6144], P(('ctx', 'ulysses')), may hold values from -120 to 120
- keys: bfloat16 [4096, 1024], P(('ctx', 'ulysses')), may hold values from -4 to 4
- values: bfloat16 [4096, 1024], P(('ctx', 'ulysses')), may hold values from -6 to 6
- doc_ids: int32 [4096], replicated, may hold values from 0 to 47, never falling along the last dimension, each value on 1 to 128 neighbouring positions
Outputs:
- attended: bfloat16 [4096, 6144], P(('ctx', 'ulysses'))
The draws below stay inside these ranges and needn't reach their ends.
Inputs may be any that keep to these rules, and one draw needn't show every extreme that they name: `doc_ids`: document numbers never fall along the tokens; every document holds at most 128 tokens and one holds exactly that many.
All inputs are finite; a program needn't handle non-finite values.
Results may differ from the reference program's by a relative error of at most 0.001.
Values may be sent and summed in bfloat16 or wider, within the bound.
No kernel may reach another device: no remote copies, remote signals or barrier semaphores. Data moves between devices by JAX's collectives and lax.ppermute only.
A program may use at most 64 MiB of HBM per device.

```python
import math
import jax
import jax.numpy as jnp
import numpy as np
from jax import lax

HQ = 48
KV = 8
HEAD = 128
BLOCK = 512
TOKENS = 4096
DOCS = 48
MOST_DOC = 128


def draw_pair(key):
    key_set = jnp.clip(jax.random.normal(jax.random.fold_in(key, 11), (TOKENS, KV, HEAD), jnp.float32), -4.0, 4.0)
    query_set = jnp.clip(jax.random.normal(jax.random.fold_in(key, 12), (TOKENS, HQ, HEAD), jnp.float32), -4.0, 4.0)
    return (query_set, key_set)


def draw_queries(key, part):
    query_set, key_set = draw_pair(key)
    return query_set.reshape(TOKENS, HQ * HEAD).astype(jnp.bfloat16)


def draw_keys(key, part):
    query_set, key_set = draw_pair(key)
    return key_set.reshape(TOKENS, KV * HEAD).astype(jnp.bfloat16)


def block_levels(key, dims, cuts, least, top_value):
    def one(position, parts):
        draws = jax.random.uniform(jax.random.fold_in(jax.random.fold_in(key, 6), position), (parts,), jnp.float32, least / len(cuts), top_value / len(cuts))
        return jnp.repeat(jnp.exp(draws), dims[position] // parts).reshape((-1,) + (1,) * (len(dims) - position - 1))

    gain = one(*cuts[0])
    for cut in cuts[1:]:
        gain = gain * one(*cut)
    return gain


def split_up(amount, total, most, slope):
    weights = [(1 << 20) // math.isqrt(rank ** slope) + 1 for rank in range(2, amount + 1)]
    spare, holding = total - most - (amount - 1), [1] * (amount - 1)
    while spare > 0:
        free = [i for i in range(amount - 1) if holding[i] < most]
        pool, left = sum([weights[i] for i in free]), spare
        for i in free:
            extra = min(most - holding[i], max(1, left * weights[i] // pool), spare)
            holding[i] = holding[i] + extra
            spare = spare - extra
    return np.array([most] + holding)


def uneven(own_key, number_of, total, bound, lean):
    if number_of == 2:
        one = jax.random.randint(own_key, (), max(1, total - bound), min(bound, total - 1) + 1)
        return jnp.stack([one, total - one])
    tallies = jnp.asarray(split_up(number_of, total, bound, lean), jnp.int32)
    twos = (number_of - 1) // 2
    source_of, taker = tallies[1:1 + 2 * twos:2], tallies[2:2 + 2 * twos:2]
    slack = jnp.minimum(source_of - 1, bound - taker)
    moved = jax.random.randint(jax.random.fold_in(own_key, 1), (twos,), 0, 1 << 20) % (slack + 1)
    tallies = tallies.at[1:1 + 2 * twos:2].set(source_of - moved).at[2:2 + 2 * twos:2].set(taker + moved)
    return tallies[jax.random.permutation(jax.random.fold_in(own_key, 2), number_of)]


def centred(stream_key, extent, spread, limit, shards=(), held_as=jnp.bfloat16):
    loudness = block_levels(stream_key, extent, shards, -0.22, 0.18) if shards else 1.0
    result = jax.random.normal(stream_key, extent, jnp.float32) * spread * loudness
    return jnp.minimum(jnp.maximum(result, -limit), limit).astype(held_as)


def setup_inputs(seed: int = 0) -> dict:
    key_list = jax.random.split(jax.random.key(seed), 5)
    queries = draw_queries(jax.random.fold_in(key_list[4], 71), 0)
    keys = draw_keys(jax.random.fold_in(key_list[4], 71), 0)
    values = centred(key_list[2], (TOKENS, KV * HEAD), 1.0, 6.0, ((0, 32),))
    doc_ids = jnp.searchsorted(jnp.cumsum(uneven(key_list[3], DOCS, TOKENS, MOST_DOC, 1)), jnp.arange(TOKENS), side="right").astype(jnp.int32)
    return dict(queries=queries, keys=keys, values=values, doc_ids=doc_ids)


def reference(queries, keys, values, doc_ids):
    scale_factor = 1.0 / math.sqrt(HEAD)
    group_size = HQ // KV
    reach = MOST_DOC
    sub_rows = 512 if TOKENS % 512 == 0 else BLOCK
    window = reach + sub_rows
    key_pad = jnp.concatenate([jnp.zeros((reach, KV * HEAD), keys.dtype), keys], axis=0)
    value_pad = jnp.concatenate([jnp.zeros((reach, KV * HEAD), values.dtype), values], axis=0)
    doc_pad = jnp.concatenate([jnp.full((reach,), -1, jnp.int32), doc_ids.astype(jnp.int32)], axis=0)

    def one_block(number):
        first_row = (number * sub_rows).astype(jnp.int32)
        query_part = lax.dynamic_slice_in_dim(queries, first_row, sub_rows, 0).reshape(sub_rows, KV, group_size, HEAD)
        key_part = lax.dynamic_slice_in_dim(key_pad, first_row, window, 0).reshape(window, KV, HEAD)
        value_part = lax.dynamic_slice_in_dim(value_pad, first_row, window, 0).reshape(window, KV, HEAD)
        query_doc = lax.dynamic_slice_in_dim(doc_ids.astype(jnp.int32), first_row, sub_rows, 0)
        key_doc = lax.dynamic_slice_in_dim(doc_pad, first_row, window, 0)
        query_pos = first_row + jnp.arange(sub_rows, dtype=jnp.int32)
        key_pos = first_row - reach + jnp.arange(window, dtype=jnp.int32)
        visible = (key_doc[None, :] == query_doc[:, None]) & (key_pos[None, :] <= query_pos[:, None])

        def one_head(operands):
            query_head, key_head, value_head = operands
            scores = jnp.einsum('bgd,wd->gbw', query_head.astype(jnp.float32), key_head.astype(jnp.float32)) * scale_factor
            scores = jnp.where(visible[None], scores, -jnp.inf)
            peak = lax.optimization_barrier(jnp.max(scores, axis=-1, keepdims=True))
            weights = jnp.exp(scores - peak)
            totals = lax.optimization_barrier(jnp.sum(weights, axis=-1))
            rounded = lax.optimization_barrier(weights.astype(jnp.bfloat16)).astype(jnp.float32)
            mixed = jnp.einsum('gbw,wd->bgd', rounded, value_head.astype(jnp.float32))
            return mixed / jnp.transpose(totals, (1, 0))[..., None]
        mixed = lax.map(one_head, (jnp.transpose(query_part, (1, 0, 2, 3)), jnp.transpose(key_part, (1, 0, 2)), jnp.transpose(value_part, (1, 0, 2))))
        return jnp.transpose(mixed, (1, 0, 2, 3)).reshape(sub_rows, HQ * HEAD).astype(jnp.bfloat16)
    blocks = lax.map(one_block, jnp.arange(TOKENS // sub_rows, dtype=jnp.int32))
    return blocks.reshape(TOKENS, HQ * HEAD)
```

```python
import functools
import math

import jax
import jax.numpy as jnp
from jax import lax
from jax.experimental import pallas as pl
from jax.experimental.pallas import tpu as pltpu
from jax.sharding import PartitionSpec as P

HQ = 48
KV = 8
HEAD = 128
PER_KV = HQ // KV
TOKENS_AXES = ("ctx", "ulysses")
HIDDEN = -1e30
EXPONENT = math.log2(math.e) / math.sqrt(HEAD)
KERNEL_VMEM = 16 * 1024 * 1024


def two_rings(count, cut):
    first = [(i, i + 1) for i in range(cut)] + [(cut, 0)]
    second = [(i, i + 1) for i in range(cut + 1, count - 1)] + [(count - 1, cut + 1)]
    return first + second


def ring(count, steps):
    return [(i, (i + steps) % count) for i in range(count)]


def swapped(count):
    return [(i, i ^ 1) for i in range(count)]


def head_columns(head):
    return pl.ds(pl.multiple_of(head * HEAD, HEAD), HEAD)


def softmax_parts(raw):
    peak = jnp.max(raw, axis=1, keepdims=True)
    weights = jnp.exp2((raw - peak) * EXPONENT)
    totals = jnp.sum(weights, axis=1, keepdims=True)
    return weights.astype(jnp.bfloat16), 1.0 / totals


def own_kernel(query, key, value, docs, early, own, cross_bias, crossing, own_bias, sems):
    length = key.shape[0]
    me = lax.axis_index(TOKENS_AXES)
    own_docs = docs[pl.ds(me, 1), :]
    before = docs[pl.ds(jnp.maximum(me - 1, 0), 1), :]
    before = jnp.where(me > 0, before, -1)
    row = lax.broadcasted_iota(jnp.int32, (length, length), 0)
    column = lax.broadcasted_iota(jnp.int32, (length, length), 1)
    row_doc = jnp.sum(jnp.where(row == column, own_docs, 0), axis=1, keepdims=True)
    own_seen = (row_doc == own_docs) & (column <= row)
    before_seen = row_doc == before
    own_bias[...] = jnp.where(own_seen, 0.0, HIDDEN)
    cross_bias[...] = jnp.where(own_seen | before_seen, 0.0, HIDDEN)
    from_before = row_doc == before[:, length - 1 :]
    crossing[...] = jnp.where(jnp.broadcast_to(from_before, (length, length)), 1.0, 0.0).astype(jnp.bfloat16)

    def group(g, carry):
        keys = key[:, head_columns(g)]
        values = value[:, head_columns(g)]
        for j in range(PER_KV):
            columns = head_columns(g * PER_KV + j)
            raw = lax.dot_general(
                query[:, columns], keys, (((1,), (1,)), ((), ())), preferred_element_type=jnp.float32
            )
            weights, share = softmax_parts(raw + own_bias[...])
            mixed = jnp.dot(weights, values, preferred_element_type=jnp.float32)
            own[:, columns] = (mixed * share).astype(jnp.bfloat16)
        return carry

    lax.fori_loop(0, KV, group, 0)


def weight_kernel(query, key, key_far, key_near, cross_bias, crossing, weights_out, share_out, *, cut):
    from_near = lax.axis_index(TOKENS_AXES) == cut + 1
    mine = crossing[...] > 0

    def group(g, carry):
        columns = head_columns(g)
        behind = jnp.where(from_near, key_near[:, columns], key_far[:, columns])
        keys = jnp.where(mine, key[:, columns], behind)
        for j in range(PER_KV):
            raw = lax.dot_general(
                query[:, head_columns(g * PER_KV + j)], keys, (((1,), (1,)), ((), ())), preferred_element_type=jnp.float32
            )
            weights, share = softmax_parts(raw + cross_bias[...])
            weights_out[g * PER_KV + j] = weights
            share_out[g * PER_KV + j] = jnp.broadcast_to(share, share_out.shape[1:])
        return carry

    lax.fori_loop(0, KV, group, 0)


def merge_kernel(weights, share, value, value_far, value_near, crossing, own, out, held, sems, *, cut):
    from_near = lax.axis_index(TOKENS_AXES) == cut + 1
    mine = crossing[...] > 0
    width = PER_KV * HEAD

    def copy(g):
        columns = pl.ds(g * width, width)
        return pltpu.make_async_copy(held.at[:, columns], out.at[:, columns], sems.at[g])

    for g in range(KV):
        columns = slice(g * HEAD, (g + 1) * HEAD)
        behind = jnp.where(from_near, value_near[:, columns], value_far[:, columns])
        values = jnp.where(mine, value[:, columns], behind)
        for j in range(PER_KV):
            head = g * PER_KV + j
            mixed = jnp.dot(weights[head], values, preferred_element_type=jnp.float32)
            fresh = (mixed * share[head]).astype(jnp.bfloat16)
            held[:, head * HEAD : (head + 1) * HEAD] = jnp.where(mine, fresh, own[:, head * HEAD : (head + 1) * HEAD])
        copy(g).start()
    for g in range(KV):
        copy(g).wait()


def in_vmem(array):
    return pltpu.with_memory_space_constraint(array, pltpu.VMEM)


def one_block_back(queries, keys, values, doc_ids):
    count = lax.axis_size(TOKENS_AXES)
    length = queries.shape[0]
    cut = count // 2 - 2
    rings, swap = two_rings(count, cut), swapped(count)
    key_near = lax.ppermute(keys, TOKENS_AXES, swap)
    key_far = lax.ppermute(keys, TOKENS_AXES, rings)
    value_near = lax.ppermute(values, TOKENS_AXES, swap)
    value_far = lax.ppermute(values, TOKENS_AXES, rings)
    docs = doc_ids.reshape(-1, length)
    whole = pl.BlockSpec(memory_space=pltpu.VMEM)
    params = pltpu.CompilerParams(vmem_limit_bytes=KERNEL_VMEM)
    square = (length, length)
    queries = in_vmem(queries)
    own, cross_bias, crossing = pl.pallas_call(
        lambda q, k, v, d, o, b, c, ob: own_kernel(q, k, v, d, None, o, b, c, ob, None),
        out_shape=(
            pltpu.VMEM(queries.shape, jnp.bfloat16),
            pltpu.VMEM(square, jnp.float32),
            pltpu.VMEM(square, jnp.bfloat16),
        ),
        in_specs=[whole] * 4,
        out_specs=[whole] * 3,
        scratch_shapes=[pltpu.VMEM(square, jnp.float32)],
        compiler_params=params,
        name="own_attention",
    )(queries, in_vmem(keys), in_vmem(values), in_vmem(docs))
    weights, share = pl.pallas_call(
        functools.partial(weight_kernel, cut=cut),
        out_shape=(
            pltpu.VMEM((HQ,) + square, jnp.bfloat16),
            pltpu.VMEM((HQ,) + square, jnp.float32),
        ),
        in_specs=[whole] * 6,
        out_specs=[whole] * 2,
        compiler_params=params,
        name="crossing_weights",
    )(queries, in_vmem(keys), in_vmem(key_far), in_vmem(key_near), cross_bias, crossing)
    return pl.pallas_call(
        functools.partial(merge_kernel, cut=cut),
        out_shape=jax.ShapeDtypeStruct(queries.shape, jnp.bfloat16),
        in_specs=[whole] * 7,
        out_specs=pl.BlockSpec(memory_space=pl.ANY),
        scratch_shapes=[pltpu.VMEM(queries.shape, jnp.bfloat16), pltpu.SemaphoreType.DMA((KV,))],
        compiler_params=params,
        name="merge",
    )(weights, share, in_vmem(values), in_vmem(value_far), in_vmem(value_near), crossing, own)


def blocks_back(queries, keys, values, doc_ids, blocks):
    count = lax.axis_size(TOKENS_AXES)
    length = queries.shape[0]
    me = lax.axis_index(TOKENS_AXES)
    halo = [
        (lax.ppermute(keys, TOKENS_AXES, ring(count, s)), lax.ppermute(values, TOKENS_AXES, ring(count, s)))
        for s in range(blocks, 0, -1)
    ] + [(keys, values)]
    window = (blocks + 1) * length
    key_all = jnp.concatenate([k for k, _ in halo], axis=0).reshape(window, KV, HEAD).transpose(1, 0, 2)
    value_all = jnp.concatenate([v for _, v in halo], axis=0).reshape(window, KV, HEAD).transpose(1, 0, 2)
    padded = jnp.concatenate([jnp.full((blocks * length,), -1, jnp.int32), doc_ids], axis=0)
    key_doc = lax.dynamic_slice_in_dim(padded, me * length, window, 0)
    query_doc = key_doc[blocks * length :]
    offset = jnp.arange(window, dtype=jnp.int32) - blocks * length
    visible = (key_doc[None, :] == query_doc[:, None]) & (offset[None, :] <= jnp.arange(length)[:, None])
    grouped = queries.reshape(length, KV, PER_KV, HEAD).transpose(1, 2, 0, 3)

    def one_head(operands):
        rows, key_rows, value_rows = operands
        raw = jnp.einsum("gqd,kd->gqk", rows, key_rows, preferred_element_type=jnp.float32)
        raw = jnp.where(visible[None], raw, HIDDEN)
        peak = jnp.max(raw, axis=-1, keepdims=True)
        weights = jnp.exp2((raw - peak) * EXPONENT)
        totals = jnp.sum(weights, axis=-1, keepdims=True)
        mixed = jnp.einsum("gqk,kd->gqd", weights.astype(jnp.bfloat16), value_rows, preferred_element_type=jnp.float32)
        return (mixed / totals).astype(jnp.bfloat16)

    mixed = lax.map(one_head, (grouped, key_all, value_all))
    return mixed.transpose(2, 0, 1, 3).reshape(length, HQ * HEAD)


def shards(queries, keys, values, doc_ids):
    length = queries.shape[0]
    reach = lax.axis_size("ulysses") * length // 4
    blocks = -(-reach // length)
    if blocks == 1 and length == HEAD:
        return one_block_back(queries, keys, values, doc_ids)
    return blocks_back(queries, keys, values, doc_ids, blocks)


def solution(mesh):
    placed = P(TOKENS_AXES, None)
    return jax.shard_map(
        shards, mesh=mesh, in_specs=(placed, placed, placed, P()), out_specs=placed, check_vma=False
    )
```

```python
import functools
import math

import jax
import jax.numpy as jnp
from jax import lax
from jax.experimental import pallas as pl
from jax.experimental.pallas import tpu as pltpu
from jax.sharding import PartitionSpec as P

HQ = 48
KV = 8
HEAD = 128
PER_KV = HQ // KV
TOKENS_AXES = ("ctx", "ulysses")
HIDDEN = -1e30
EXPONENT = math.log2(math.e) / math.sqrt(HEAD)
KERNEL_VMEM = 16 * 1024 * 1024


def two_rings(count, cut):
    first = [(i, i + 1) for i in range(cut)] + [(cut, 0)]
    second = [(i, i + 1) for i in range(cut + 1, count - 1)] + [(count - 1, cut + 1)]
    return first + second


def ring(count, steps):
    return [(i, (i + steps) % count) for i in range(count)]


def swapped(count):
    return [(i, i ^ 1) for i in range(count)]


def head_columns(head, heads=1):
    return slice(head * HEAD, (head + heads) * HEAD)


def column_softmax(raw):
    peak = jnp.max(raw, axis=0, keepdims=True)
    weights = jnp.exp2((raw - peak) * EXPONENT)
    return weights, 1.0 / jnp.sum(weights, axis=0, keepdims=True)


def raw_scores(keys, query, head, bias):
    raw = lax.dot_general(
        keys,
        jnp.concatenate([query[:, head_columns(head)], query[:, head_columns(head + 1)]], axis=0),
        (((1,), (1,)), ((), ())),
        preferred_element_type=jnp.float32,
    )
    return raw + jnp.concatenate([bias, bias], axis=1)


def own_kernel(
    query_in, key_in, value_in, docs_in, own, query, key, value, cross_bias, crossing, own_bias, docs, sems
):
    length = key.shape[0]
    width = PER_KV * HEAD
    pieces = [(docs_in, docs), (key_in, key)]
    pieces += [(query_in.at[:, g * width : (g + 1) * width], query.at[:, g * width : (g + 1) * width]) for g in range(KV)]
    pieces.insert(3, (value_in, value))
    copies = [pltpu.make_async_copy(source, target, sems.at[i]) for i, (source, target) in enumerate(pieces)]
    for copy in copies:
        copy.start()
    copies[0].wait()
    me = lax.axis_index(TOKENS_AXES)
    own_docs = docs[pl.ds(me, 1), :]
    before = jnp.where(me > 0, docs[pl.ds(jnp.maximum(me - 1, 0), 1), :], -1)
    row = lax.broadcasted_iota(jnp.int32, (length, length), 0)
    column = lax.broadcasted_iota(jnp.int32, (length, length), 1)
    diagonal = row == column
    key_doc = jnp.sum(jnp.where(diagonal, own_docs, 0), axis=1, keepdims=True)
    before_doc = jnp.sum(jnp.where(diagonal, before, 0), axis=1, keepdims=True)
    own_seen = (key_doc == own_docs) & (row <= column)
    own_bias[...] = jnp.where(own_seen, 0.0, HIDDEN)
    cross_bias[...] = jnp.where(own_seen | (before_doc == own_docs), 0.0, HIDDEN)
    crossing[...] = jnp.where(key_doc == before[:, length - 1 :], jnp.ones((length, length), jnp.float32), 0.0).astype(
        jnp.bfloat16
    )
    copies[1].wait()
    for g in range(KV):
        copies[2 if g == 0 else g + 3].wait()
        if g == 0:
            copies[3].wait()
        keys = key[:, head_columns(g)]
        values = value[:, head_columns(g)].T
        for head in range(g * PER_KV, (g + 1) * PER_KV, 2):
            weights, share = column_softmax(raw_scores(keys, query, head, own_bias[...]))
            mixed = jnp.dot(values, weights.astype(jnp.bfloat16), preferred_element_type=jnp.float32)
            mixed = (mixed * share).astype(jnp.bfloat16)
            own[:, head_columns(head)] = mixed[:, :length].T
            own[:, head_columns(head + 1)] = mixed[:, length:].T


def weight_kernel(query, key, key_far, key_near, cross_bias, crossing, weights_out, share_out, *, cut):
    length = key.shape[0]
    from_near = lax.axis_index(TOKENS_AXES) == cut + 1
    mine = crossing[...] > 0
    for g in range(KV):
        columns = head_columns(g)
        behind = jnp.where(from_near, key_near[:, columns], key_far[:, columns])
        keys = jnp.where(mine, key[:, columns], behind)
        for head in range(g * PER_KV, (g + 1) * PER_KV, 2):
            weights, share = column_softmax(raw_scores(keys, query, head, cross_bias[...]))
            weights = weights.astype(jnp.bfloat16)
            for i in range(2):
                part = slice(i * length, (i + 1) * length)
                weights_out[head + i] = weights[:, part].T
                share_out[head + i] = jnp.broadcast_to(share[:, part], (HEAD, length)).T


def merge_kernel(weights, share, value, value_far, value_near, crossing, own, out, held, sems, *, cut):
    from_near = lax.axis_index(TOKENS_AXES) == cut + 1
    mine = crossing[...] > 0
    copies = []
    for g in range(KV):
        columns = head_columns(g)
        behind = jnp.where(from_near, value_near[:, columns], value_far[:, columns])
        values = jnp.where(mine, value[:, columns], behind)
        for head in range(g * PER_KV, (g + 1) * PER_KV):
            mixed = jnp.dot(weights[head], values, preferred_element_type=jnp.float32)
            fresh = (mixed * share[head]).astype(jnp.bfloat16)
            held[:, head_columns(head)] = jnp.where(mine, fresh, own[:, head_columns(head)])
        group = head_columns(g * PER_KV, PER_KV)
        copies.append(pltpu.make_async_copy(held.at[:, group], out.at[:, group], sems.at[g]))
        copies[-1].start()
    for copy in copies:
        copy.wait()


def in_vmem(array):
    return pltpu.with_memory_space_constraint(array, pltpu.VMEM)


def one_block_back(queries, keys, values, doc_ids):
    count = lax.axis_size(TOKENS_AXES)
    length = queries.shape[0]
    cut = count // 2 - 2
    rings, swap = two_rings(count, cut), swapped(count)
    key_far = lax.ppermute(keys, TOKENS_AXES, rings)
    key_near = lax.ppermute(keys, TOKENS_AXES, swap)
    value_far = lax.ppermute(values, TOKENS_AXES, rings)
    value_near = lax.ppermute(values, TOKENS_AXES, swap)
    docs = doc_ids.reshape(-1, length)
    whole = pl.BlockSpec(memory_space=pltpu.VMEM)
    anywhere = pl.BlockSpec(memory_space=pl.ANY)
    params = pltpu.CompilerParams(vmem_limit_bytes=KERNEL_VMEM)
    square = (length, length)
    own, query_held, key_held, value_held, cross_bias, crossing = pl.pallas_call(
        own_kernel,
        out_shape=(
            pltpu.VMEM(queries.shape, jnp.bfloat16),
            pltpu.VMEM(queries.shape, jnp.bfloat16),
            pltpu.VMEM(keys.shape, jnp.bfloat16),
            pltpu.VMEM(values.shape, jnp.bfloat16),
            pltpu.VMEM(square, jnp.float32),
            pltpu.VMEM(square, jnp.bfloat16),
        ),
        in_specs=[pl.BlockSpec(memory_space=pltpu.HBM)] * 4,
        out_specs=[whole] * 6,
        scratch_shapes=[
            pltpu.VMEM(square, jnp.float32),
            pltpu.VMEM(docs.shape, jnp.int32),
            pltpu.SemaphoreType.DMA((KV + 3,)),
        ],
        compiler_params=params,
        name="own_attention",
    )(*(pltpu.with_memory_space_constraint(array, pltpu.HBM) for array in (queries, keys, values, docs)))
    weights, share = pl.pallas_call(
        functools.partial(weight_kernel, cut=cut),
        out_shape=(
            pltpu.VMEM((HQ,) + square, jnp.bfloat16),
            pltpu.VMEM((HQ,) + square, jnp.float32),
        ),
        in_specs=[whole] * 6,
        out_specs=[whole] * 2,
        compiler_params=params,
        name="crossing_weights",
    )(query_held, key_held, in_vmem(key_far), in_vmem(key_near), cross_bias, crossing)
    return pl.pallas_call(
        functools.partial(merge_kernel, cut=cut),
        out_shape=jax.ShapeDtypeStruct(queries.shape, jnp.bfloat16),
        in_specs=[whole] * 7,
        out_specs=anywhere,
        scratch_shapes=[pltpu.VMEM(queries.shape, jnp.bfloat16), pltpu.SemaphoreType.DMA((KV,))],
        compiler_params=params,
        name="merge",
    )(weights, share, value_held, in_vmem(value_far), in_vmem(value_near), crossing, own)


def blocks_back(queries, keys, values, doc_ids, blocks):
    count = lax.axis_size(TOKENS_AXES)
    length = queries.shape[0]
    me = lax.axis_index(TOKENS_AXES)
    halo = [
        (lax.ppermute(keys, TOKENS_AXES, ring(count, s)), lax.ppermute(values, TOKENS_AXES, ring(count, s)))
        for s in range(blocks, 0, -1)
    ] + [(keys, values)]
    window = (blocks + 1) * length
    key_all = jnp.concatenate([k for k, _ in halo], axis=0).reshape(window, KV, HEAD).transpose(1, 0, 2)
    value_all = jnp.concatenate([v for _, v in halo], axis=0).reshape(window, KV, HEAD).transpose(1, 0, 2)
    padded = jnp.concatenate([jnp.full((blocks * length,), -1, jnp.int32), doc_ids], axis=0)
    key_doc = lax.dynamic_slice_in_dim(padded, me * length, window, 0)
    query_doc = key_doc[blocks * length :]
    offset = jnp.arange(window, dtype=jnp.int32) - blocks * length
    visible = (key_doc[None, :] == query_doc[:, None]) & (offset[None, :] <= jnp.arange(length)[:, None])
    grouped = queries.reshape(length, KV, PER_KV, HEAD).transpose(1, 2, 0, 3)

    def one_head(operands):
        rows, key_rows, value_rows = operands
        raw = jnp.einsum("gqd,kd->gqk", rows, key_rows, preferred_element_type=jnp.float32)
        raw = jnp.where(visible[None], raw, HIDDEN)
        peak = jnp.max(raw, axis=-1, keepdims=True)
        weights = jnp.exp2((raw - peak) * EXPONENT)
        totals = jnp.sum(weights, axis=-1, keepdims=True)
        mixed = jnp.einsum("gqk,kd->gqd", weights.astype(jnp.bfloat16), value_rows, preferred_element_type=jnp.float32)
        return (mixed / totals).astype(jnp.bfloat16)

    mixed = lax.map(one_head, (grouped, key_all, value_all))
    return mixed.transpose(2, 0, 1, 3).reshape(length, HQ * HEAD)


def shards(queries, keys, values, doc_ids):
    length = queries.shape[0]
    reach = lax.axis_size("ulysses") * length // 4
    blocks = -(-reach // length)
    if blocks == 1 and length == HEAD:
        return one_block_back(queries, keys, values, doc_ids)
    return blocks_back(queries, keys, values, doc_ids, blocks)


def solution(mesh):
    placed = P(TOKENS_AXES, None)
    return jax.shard_map(
        shards, mesh=mesh, in_specs=(placed, placed, placed, P()), out_specs=placed, check_vma=False
    )
```

```python
import functools
import math

import jax
import jax.numpy as jnp
from jax import lax
from jax.experimental import pallas as pl
from jax.experimental.pallas import tpu as pltpu
from jax.sharding import PartitionSpec as P

HQ = 48
KV = 8
HEAD = 128
PER_KV = HQ // KV
TOKENS_AXES = ("ctx", "ulysses")
HIDDEN = -1e30
EXPONENT = math.log2(math.e) / math.sqrt(HEAD)
KERNEL_VMEM = 16 * 1024 * 1024


def two_rings(count, cut):
    first = [(i, i + 1) for i in range(cut)] + [(cut, 0)]
    second = [(i, i + 1) for i in range(cut + 1, count - 1)] + [(count - 1, cut + 1)]
    return first + second


def ring(count, steps):
    return [(i, (i + steps) % count) for i in range(count)]


def swapped(count):
    return [(i, i ^ 1) for i in range(count)]


def head_columns(head, heads=1):
    return slice(head * HEAD, (head + heads) * HEAD)


def column_softmax(raw):
    peak = jnp.max(raw, axis=0, keepdims=True)
    weights = jnp.exp2((raw - peak) * EXPONENT)
    return weights, 1.0 / jnp.sum(weights, axis=0, keepdims=True)


def raw_scores(keys, query, head, bias):
    raw = lax.dot_general(
        keys,
        jnp.concatenate([query[:, head_columns(head)], query[:, head_columns(head + 1)]], axis=0),
        (((1,), (1,)), ((), ())),
        preferred_element_type=jnp.float32,
    )
    return raw + jnp.concatenate([bias, bias], axis=1)


def own_kernel(
    query_in, key_in, value_in, docs_in, own, query, key, value, cross_bias, crossing, own_bias, docs, sems
):
    length = key.shape[0]
    width = PER_KV * HEAD
    pieces = [(docs_in, docs), (key_in, key), (value_in, value)]
    pieces += [(query_in.at[:, g * width : (g + 1) * width], query.at[:, g * width : (g + 1) * width]) for g in range(KV)]
    copies = [pltpu.make_async_copy(source, target, sems.at[i]) for i, (source, target) in enumerate(pieces)]
    for copy in copies:
        copy.start()
    copies[0].wait()
    me = lax.axis_index(TOKENS_AXES)
    own_docs = docs[pl.ds(me, 1), :]
    before = jnp.where(me > 0, docs[pl.ds(jnp.maximum(me - 1, 0), 1), :], -1)
    row = lax.broadcasted_iota(jnp.int32, (length, length), 0)
    column = lax.broadcasted_iota(jnp.int32, (length, length), 1)
    diagonal = row == column
    key_doc = jnp.sum(jnp.where(diagonal, own_docs, 0), axis=1, keepdims=True)
    before_doc = jnp.sum(jnp.where(diagonal, before, 0), axis=1, keepdims=True)
    own_seen = (key_doc == own_docs) & (row <= column)
    own_bias[...] = jnp.where(own_seen, 0.0, HIDDEN)
    cross_bias[...] = jnp.where(own_seen | (before_doc == own_docs), 0.0, HIDDEN)
    crossing[...] = jnp.where(key_doc == before[:, length - 1 :], jnp.ones((length, length), jnp.float32), 0.0).astype(
        jnp.bfloat16
    )
    for copy in copies[1:]:
        copy.wait()
    for g in range(KV):
        keys = key[:, head_columns(g)]
        values = value[:, head_columns(g)].T
        for head in range(g * PER_KV, (g + 1) * PER_KV, 2):
            weights, share = column_softmax(raw_scores(keys, query, head, own_bias[...]))
            mixed = jnp.dot(values, weights.astype(jnp.bfloat16), preferred_element_type=jnp.float32)
            mixed = (mixed * share).astype(jnp.bfloat16)
            own[:, head_columns(head)] = mixed[:, :length].T
            own[:, head_columns(head + 1)] = mixed[:, length:].T


def weight_kernel(query, key, key_far, key_near, cross_bias, crossing, weights_out, share_out, *, cut):
    length = key.shape[0]
    from_near = lax.axis_index(TOKENS_AXES) == cut + 1
    mine = crossing[...] > 0
    for g in range(KV):
        columns = head_columns(g)
        behind = jnp.where(from_near, key_near[:, columns], key_far[:, columns])
        keys = jnp.where(mine, key[:, columns], behind)
        for head in range(g * PER_KV, (g + 1) * PER_KV, 2):
            weights, share = column_softmax(raw_scores(keys, query, head, cross_bias[...]))
            weights = weights.astype(jnp.bfloat16)
            for i in range(2):
                part = slice(i * length, (i + 1) * length)
                weights_out[head + i] = weights[:, part].T
                share_out[head + i] = jnp.broadcast_to(share[:, part], (HEAD, length)).T


def merge_kernel(weights, share, value, value_far, value_near, crossing, own, out, held, sems, *, cut):
    from_near = lax.axis_index(TOKENS_AXES) == cut + 1
    mine = crossing[...] > 0
    copies = []
    for g in range(KV):
        columns = head_columns(g)
        behind = jnp.where(from_near, value_near[:, columns], value_far[:, columns])
        values = jnp.where(mine, value[:, columns], behind)
        for head in range(g * PER_KV, (g + 1) * PER_KV):
            mixed = jnp.dot(weights[head], values, preferred_element_type=jnp.float32)
            fresh = (mixed * share[head]).astype(jnp.bfloat16)
            held[:, head_columns(head)] = jnp.where(mine, fresh, own[:, head_columns(head)])
        group = head_columns(g * PER_KV, PER_KV)
        copies.append(pltpu.make_async_copy(held.at[:, group], out.at[:, group], sems.at[g]))
        copies[-1].start()
    for copy in copies:
        copy.wait()


def in_vmem(array):
    return pltpu.with_memory_space_constraint(array, pltpu.VMEM)


def one_block_back(queries, keys, values, doc_ids):
    count = lax.axis_size(TOKENS_AXES)
    length = queries.shape[0]
    cut = count // 2 - 2
    rings, swap = two_rings(count, cut), swapped(count)
    key_near = lax.ppermute(keys, TOKENS_AXES, swap)
    value_near = lax.ppermute(values, TOKENS_AXES, swap)
    key_far = lax.ppermute(keys, TOKENS_AXES, rings)
    value_far = lax.ppermute(values, TOKENS_AXES, rings)
    docs = doc_ids.reshape(-1, length)
    whole = pl.BlockSpec(memory_space=pltpu.VMEM)
    anywhere = pl.BlockSpec(memory_space=pl.ANY)
    params = pltpu.CompilerParams(vmem_limit_bytes=KERNEL_VMEM)
    square = (length, length)
    own, query_held, key_held, value_held, cross_bias, crossing = pl.pallas_call(
        own_kernel,
        out_shape=(
            pltpu.VMEM(queries.shape, jnp.bfloat16),
            pltpu.VMEM(queries.shape, jnp.bfloat16),
            pltpu.VMEM(keys.shape, jnp.bfloat16),
            pltpu.VMEM(values.shape, jnp.bfloat16),
            pltpu.VMEM(square, jnp.float32),
            pltpu.VMEM(square, jnp.bfloat16),
        ),
        in_specs=[pl.BlockSpec(memory_space=pltpu.HBM)] * 4,
        out_specs=[whole] * 6,
        scratch_shapes=[
            pltpu.VMEM(square, jnp.float32),
            pltpu.VMEM(docs.shape, jnp.int32),
            pltpu.SemaphoreType.DMA((KV + 3,)),
        ],
        compiler_params=params,
        name="own_attention",
    )(*(pltpu.with_memory_space_constraint(array, pltpu.HBM) for array in (queries, keys, values, docs)))
    weights, share = pl.pallas_call(
        functools.partial(weight_kernel, cut=cut),
        out_shape=(
            pltpu.VMEM((HQ,) + square, jnp.bfloat16),
            pltpu.VMEM((HQ,) + square, jnp.float32),
        ),
        in_specs=[whole] * 6,
        out_specs=[whole] * 2,
        compiler_params=params,
        name="crossing_weights",
    )(query_held, key_held, in_vmem(key_far), in_vmem(key_near), cross_bias, crossing)
    return pl.pallas_call(
        functools.partial(merge_kernel, cut=cut),
        out_shape=jax.ShapeDtypeStruct(queries.shape, jnp.bfloat16),
        in_specs=[whole] * 7,
        out_specs=anywhere,
        scratch_shapes=[pltpu.VMEM(queries.shape, jnp.bfloat16), pltpu.SemaphoreType.DMA((KV,))],
        compiler_params=params,
        name="merge",
    )(weights, share, value_held, in_vmem(value_far), in_vmem(value_near), crossing, own)


def blocks_back(queries, keys, values, doc_ids, blocks):
    count = lax.axis_size(TOKENS_AXES)
    length = queries.shape[0]
    me = lax.axis_index(TOKENS_AXES)
    halo = [
        (lax.ppermute(keys, TOKENS_AXES, ring(count, s)), lax.ppermute(values, TOKENS_AXES, ring(count, s)))
        for s in range(blocks, 0, -1)
    ] + [(keys, values)]
    window = (blocks + 1) * length
    key_all = jnp.concatenate([k for k, _ in halo], axis=0).reshape(window, KV, HEAD).transpose(1, 0, 2)
    value_all = jnp.concatenate([v for _, v in halo], axis=0).reshape(window, KV, HEAD).transpose(1, 0, 2)
    padded = jnp.concatenate([jnp.full((blocks * length,), -1, jnp.int32), doc_ids], axis=0)
    key_doc = lax.dynamic_slice_in_dim(padded, me * length, window, 0)
    query_doc = key_doc[blocks * length :]
    offset = jnp.arange(window, dtype=jnp.int32) - blocks * length
    visible = (key_doc[None, :] == query_doc[:, None]) & (offset[None, :] <= jnp.arange(length)[:, None])
    grouped = queries.reshape(length, KV, PER_KV, HEAD).transpose(1, 2, 0, 3)

    def one_head(operands):
        rows, key_rows, value_rows = operands
        raw = jnp.einsum("gqd,kd->gqk", rows, key_rows, preferred_element_type=jnp.float32)
        raw = jnp.where(visible[None], raw, HIDDEN)
        peak = jnp.max(raw, axis=-1, keepdims=True)
        weights = jnp.exp2((raw - peak) * EXPONENT)
        totals = jnp.sum(weights, axis=-1, keepdims=True)
        mixed = jnp.einsum("gqk,kd->gqd", weights.astype(jnp.bfloat16), value_rows, preferred_element_type=jnp.float32)
        return (mixed / totals).astype(jnp.bfloat16)

    mixed = lax.map(one_head, (grouped, key_all, value_all))
    return mixed.transpose(2, 0, 1, 3).reshape(length, HQ * HEAD)


def shards(queries, keys, values, doc_ids):
    length = queries.shape[0]
    reach = lax.axis_size("ulysses") * length // 4
    blocks = -(-reach // length)
    if blocks == 1 and length == HEAD:
        return one_block_back(queries, keys, values, doc_ids)
    return blocks_back(queries, keys, values, doc_ids, blocks)


def solution(mesh):
    placed = P(TOKENS_AXES, None)
    return jax.shard_map(
        shards, mesh=mesh, in_specs=(placed, placed, placed, P()), out_specs=placed, check_vma=False
    )
```

```python
import functools
import math

import jax
import jax.numpy as jnp
from jax import lax
from jax.experimental import pallas as pl
from jax.experimental.pallas import tpu as pltpu
from jax.sharding import PartitionSpec as P

HQ = 48
KV = 8
HEAD = 128
PER_KV = HQ // KV
TOKENS_AXES = ("ctx", "ulysses")
HIDDEN = -1e30
EXPONENT = math.log2(math.e) / math.sqrt(HEAD)
KERNEL_VMEM = 16 * 1024 * 1024


def cuts_of(count):
    return [cut for cut in [4, 6] + list(range(14, count, 8)) if cut < count - 2]


def rings_between(count, cuts):
    pairs, first = [], 0
    for last in cuts + [count - 1]:
        pairs += [(i, i + 1) for i in range(first, last)] + [(last, first)]
        first = last + 1
    return pairs


def after_cut(cuts):
    me = lax.axis_index(TOKENS_AXES)
    return functools.reduce(jnp.logical_or, [me == cut + 1 for cut in cuts], False)


def ring(count, steps):
    return [(i, (i + steps) % count) for i in range(count)]


def swapped(count):
    return [(i, i ^ 1) for i in range(count)]


def head_columns(head, heads=1):
    return slice(head * HEAD, (head + heads) * HEAD)


def column_softmax(raw):
    peak = jnp.max(raw, axis=0, keepdims=True)
    weights = jnp.exp2((raw - peak) * EXPONENT)
    return weights, 1.0 / jnp.sum(weights, axis=0, keepdims=True)


def raw_scores(keys, query, head, bias):
    raw = lax.dot_general(
        keys,
        jnp.concatenate([query[:, head_columns(head)], query[:, head_columns(head + 1)]], axis=0),
        (((1,), (1,)), ((), ())),
        preferred_element_type=jnp.float32,
    )
    return raw + jnp.concatenate([bias, bias], axis=1)


def own_kernel(
    query_in, key_in, value_in, docs_in, own, query, key, value, cross_bias, crossing, own_bias, docs, sems
):
    length = key.shape[0]
    width = PER_KV * HEAD
    pieces = [(docs_in, docs), (key_in, key), (value_in, value)]
    pieces += [(query_in.at[:, g * width : (g + 1) * width], query.at[:, g * width : (g + 1) * width]) for g in range(KV)]
    copies = [pltpu.make_async_copy(source, target, sems.at[i]) for i, (source, target) in enumerate(pieces)]
    for copy in copies:
        copy.start()
    copies[0].wait()
    me = lax.axis_index(TOKENS_AXES)
    own_docs = docs[pl.ds(me, 1), :]
    before = jnp.where(me > 0, docs[pl.ds(jnp.maximum(me - 1, 0), 1), :], -1)
    row = lax.broadcasted_iota(jnp.int32, (length, length), 0)
    column = lax.broadcasted_iota(jnp.int32, (length, length), 1)
    diagonal = row == column
    key_doc = jnp.sum(jnp.where(diagonal, own_docs, 0), axis=1, keepdims=True)
    before_doc = jnp.sum(jnp.where(diagonal, before, 0), axis=1, keepdims=True)
    own_seen = (key_doc == own_docs) & (row <= column)
    own_bias[...] = jnp.where(own_seen, 0.0, HIDDEN)
    cross_bias[...] = jnp.where(own_seen | (before_doc == own_docs), 0.0, HIDDEN)
    crossing[...] = jnp.where(key_doc == before[:, length - 1 :], jnp.ones((length, length), jnp.float32), 0.0).astype(
        jnp.bfloat16
    )
    for copy in copies[1:]:
        copy.wait()
    for g in range(KV):
        keys = key[:, head_columns(g)]
        values = value[:, head_columns(g)].T
        for head in range(g * PER_KV, (g + 1) * PER_KV, 2):
            weights, share = column_softmax(raw_scores(keys, query, head, own_bias[...]))
            mixed = jnp.dot(values, weights.astype(jnp.bfloat16), preferred_element_type=jnp.float32)
            mixed = (mixed * share).astype(jnp.bfloat16)
            own[:, head_columns(head)] = mixed[:, :length].T
            own[:, head_columns(head + 1)] = mixed[:, length:].T


def weight_kernel(query, key, key_near, key_far, cross_bias, crossing, weights_out, share_out, *, cuts):
    length = key.shape[0]
    from_near = after_cut(cuts)
    mine = crossing[...] > 0
    for g in range(KV):
        columns = head_columns(g)
        behind = jnp.where(from_near, key_near[:, columns], key_far[:, columns])
        keys = jnp.where(mine, key[:, columns], behind)
        for head in range(g * PER_KV, (g + 1) * PER_KV, 2):
            weights, share = column_softmax(raw_scores(keys, query, head, cross_bias[...]))
            weights = weights.astype(jnp.bfloat16)
            for i in range(2):
                part = slice(i * length, (i + 1) * length)
                weights_out[head + i] = weights[:, part].T
                share_out[head + i] = jnp.broadcast_to(share[:, part], (HEAD, length)).T


def merge_kernel(weights, share, value, value_far, value_near, crossing, own, out, held, sems, *, cuts):
    from_near = after_cut(cuts)
    mine = crossing[...] > 0
    copies = []
    for g in range(KV):
        columns = head_columns(g)
        behind = jnp.where(from_near, value_near[:, columns], value_far[:, columns])
        values = jnp.where(mine, value[:, columns], behind)
        for head in range(g * PER_KV, (g + 1) * PER_KV):
            mixed = jnp.dot(weights[head], values, preferred_element_type=jnp.float32)
            fresh = (mixed * share[head]).astype(jnp.bfloat16)
            held[:, head_columns(head)] = jnp.where(mine, fresh, own[:, head_columns(head)])
        group = head_columns(g * PER_KV, PER_KV)
        copies.append(pltpu.make_async_copy(held.at[:, group], out.at[:, group], sems.at[g]))
        copies[-1].start()
    for copy in copies:
        copy.wait()


def in_vmem(array):
    return pltpu.with_memory_space_constraint(array, pltpu.VMEM)


def one_block_back(queries, keys, values, doc_ids):
    count = lax.axis_size(TOKENS_AXES)
    length = queries.shape[0]
    cuts = cuts_of(count)
    rings, swap = rings_between(count, cuts), swapped(count)
    key_near = lax.ppermute(keys, TOKENS_AXES, swap)
    key_far = lax.ppermute(keys, TOKENS_AXES, rings)
    value_near = lax.ppermute(values, TOKENS_AXES, swap)
    value_far = lax.ppermute(values, TOKENS_AXES, rings)
    docs = doc_ids.reshape(-1, length)
    whole = pl.BlockSpec(memory_space=pltpu.VMEM)
    anywhere = pl.BlockSpec(memory_space=pl.ANY)
    params = pltpu.CompilerParams(vmem_limit_bytes=KERNEL_VMEM)
    square = (length, length)
    own, query_held, key_held, value_held, cross_bias, crossing = pl.pallas_call(
        own_kernel,
        out_shape=(
            pltpu.VMEM(queries.shape, jnp.bfloat16),
            pltpu.VMEM(queries.shape, jnp.bfloat16),
            pltpu.VMEM(keys.shape, jnp.bfloat16),
            pltpu.VMEM(values.shape, jnp.bfloat16),
            pltpu.VMEM(square, jnp.float32),
            pltpu.VMEM(square, jnp.bfloat16),
        ),
        in_specs=[pl.BlockSpec(memory_space=pltpu.HBM)] * 4,
        out_specs=[whole] * 6,
        scratch_shapes=[
            pltpu.VMEM(square, jnp.float32),
            pltpu.VMEM(docs.shape, jnp.int32),
            pltpu.SemaphoreType.DMA((KV + 3,)),
        ],
        compiler_params=params,
        name="own_attention",
    )(*(pltpu.with_memory_space_constraint(array, pltpu.HBM) for array in (queries, keys, values, docs)))
    weights, share = pl.pallas_call(
        functools.partial(weight_kernel, cuts=cuts),
        out_shape=(
            pltpu.VMEM((HQ,) + square, jnp.bfloat16),
            pltpu.VMEM((HQ,) + square, jnp.float32),
        ),
        in_specs=[whole] * 6,
        out_specs=[whole] * 2,
        compiler_params=params,
        name="crossing_weights",
    )(query_held, key_held, in_vmem(key_near), in_vmem(key_far), cross_bias, crossing)
    return pl.pallas_call(
        functools.partial(merge_kernel, cuts=cuts),
        out_shape=jax.ShapeDtypeStruct(queries.shape, jnp.bfloat16),
        in_specs=[whole] * 7,
        out_specs=anywhere,
        scratch_shapes=[pltpu.VMEM(queries.shape, jnp.bfloat16), pltpu.SemaphoreType.DMA((KV,))],
        compiler_params=params,
        name="merge",
    )(weights, share, value_held, in_vmem(value_far), in_vmem(value_near), crossing, own)


def blocks_back(queries, keys, values, doc_ids, blocks):
    count = lax.axis_size(TOKENS_AXES)
    length = queries.shape[0]
    me = lax.axis_index(TOKENS_AXES)
    halo = [
        (lax.ppermute(keys, TOKENS_AXES, ring(count, s)), lax.ppermute(values, TOKENS_AXES, ring(count, s)))
        for s in range(blocks, 0, -1)
    ] + [(keys, values)]
    window = (blocks + 1) * length
    key_all = jnp.concatenate([k for k, _ in halo], axis=0).reshape(window, KV, HEAD).transpose(1, 0, 2)
    value_all = jnp.concatenate([v for _, v in halo], axis=0).reshape(window, KV, HEAD).transpose(1, 0, 2)
    padded = jnp.concatenate([jnp.full((blocks * length,), -1, jnp.int32), doc_ids], axis=0)
    key_doc = lax.dynamic_slice_in_dim(padded, me * length, window, 0)
    query_doc = key_doc[blocks * length :]
    offset = jnp.arange(window, dtype=jnp.int32) - blocks * length
    visible = (key_doc[None, :] == query_doc[:, None]) & (offset[None, :] <= jnp.arange(length)[:, None])
    grouped = queries.reshape(length, KV, PER_KV, HEAD).transpose(1, 2, 0, 3)

    def one_head(operands):
        rows, key_rows, value_rows = operands
        raw = jnp.einsum("gqd,kd->gqk", rows, key_rows, preferred_element_type=jnp.float32)
        raw = jnp.where(visible[None], raw, HIDDEN)
        peak = jnp.max(raw, axis=-1, keepdims=True)
        weights = jnp.exp2((raw - peak) * EXPONENT)
        totals = jnp.sum(weights, axis=-1, keepdims=True)
        mixed = jnp.einsum("gqk,kd->gqd", weights.astype(jnp.bfloat16), value_rows, preferred_element_type=jnp.float32)
        return (mixed / totals).astype(jnp.bfloat16)

    mixed = lax.map(one_head, (grouped, key_all, value_all))
    return mixed.transpose(2, 0, 1, 3).reshape(length, HQ * HEAD)


def shards(queries, keys, values, doc_ids):
    length = queries.shape[0]
    reach = lax.axis_size("ulysses") * length // 4
    blocks = -(-reach // length)
    if blocks == 1 and length == HEAD:
        return one_block_back(queries, keys, values, doc_ids)
    return blocks_back(queries, keys, values, doc_ids, blocks)


def solution(mesh):
    placed = P(TOKENS_AXES, None)
    return jax.shard_map(
        shards, mesh=mesh, in_specs=(placed, placed, placed, P()), out_specs=placed, check_vma=False
    )
```

```python
import functools
import math

import jax
import jax.numpy as jnp
from jax import lax
from jax.experimental import pallas as pl
from jax.experimental.pallas import tpu as pltpu
from jax.sharding import PartitionSpec as P

HQ = 48
KV = 8
HEAD = 128
PER_KV = HQ // KV
TOKENS_AXES = ("ctx", "ulysses")
HIDDEN = -1e30
EXPONENT = math.log2(math.e) / math.sqrt(HEAD)
KERNEL_VMEM = 16 * 1024 * 1024


def cuts_of(count):
    return [cut for cut in [4, 6] + list(range(14, count, 8)) if cut < count - 2]


def rings_between(count, cuts):
    pairs, first = [], 0
    for last in cuts + [count - 1]:
        pairs += [(i, i + 1) for i in range(first, last)] + [(last, first)]
        first = last + 1
    return pairs


def after_cut(cuts):
    me = lax.axis_index(TOKENS_AXES)
    return functools.reduce(jnp.logical_or, [me == cut + 1 for cut in cuts], False)


def ring(count, steps):
    return [(i, (i + steps) % count) for i in range(count)]


def swapped(count):
    return [(i, i ^ 1) for i in range(count)]


def head_columns(head, heads=1):
    return slice(head * HEAD, (head + heads) * HEAD)


def column_softmax(raw):
    peak = jnp.max(raw, axis=0, keepdims=True)
    weights = jnp.exp2((raw - peak) * EXPONENT)
    return weights, 1.0 / jnp.sum(weights, axis=0, keepdims=True)


def raw_scores(keys, query, head, bias):
    raw = lax.dot_general(
        keys,
        jnp.concatenate([query[:, head_columns(head)], query[:, head_columns(head + 1)]], axis=0),
        (((1,), (1,)), ((), ())),
        preferred_element_type=jnp.float32,
    )
    return raw + jnp.concatenate([bias, bias], axis=1)


def own_kernel(
    query_in,
    key_in,
    value_in,
    docs_in,
    own,
    query,
    key,
    value,
    cross_bias,
    crossing,
    own_bias,
    docs,
    docs_sem,
    key_sem,
    value_sem,
    query_sem,
):
    length = key.shape[0]
    docs_copy = pltpu.make_async_copy(docs_in, docs, docs_sem)
    pieces = [(key_in, key, key_sem), (value_in, value, value_sem), (query_in, query, query_sem)]
    copies = [pltpu.make_async_copy(source, target, sem) for source, target, sem in pieces]
    docs_copy.start()
    for copy in copies:
        copy.start()
    docs_copy.wait()
    me = lax.axis_index(TOKENS_AXES)
    own_docs = docs[pl.ds(me, 1), :]
    before = jnp.where(me > 0, docs[pl.ds(jnp.maximum(me - 1, 0), 1), :], -1)
    row = lax.broadcasted_iota(jnp.int32, (length, length), 0)
    column = lax.broadcasted_iota(jnp.int32, (length, length), 1)
    diagonal = row == column
    key_doc = jnp.sum(jnp.where(diagonal, own_docs, 0), axis=1, keepdims=True)
    before_doc = jnp.sum(jnp.where(diagonal, before, 0), axis=1, keepdims=True)
    own_seen = (key_doc == own_docs) & (row <= column)
    own_bias[...] = jnp.where(own_seen, 0.0, HIDDEN)
    cross_bias[...] = jnp.where(own_seen | (before_doc == own_docs), 0.0, HIDDEN)
    crossing[...] = jnp.where(key_doc == before[:, length - 1 :], jnp.ones((length, length), jnp.float32), 0.0).astype(
        jnp.bfloat16
    )
    for copy in copies:
        copy.wait()
    for g in range(KV):
        keys = key[:, head_columns(g)]
        values = value[:, head_columns(g)].T
        for head in range(g * PER_KV, (g + 1) * PER_KV, 2):
            weights, share = column_softmax(raw_scores(keys, query, head, own_bias[...]))
            mixed = jnp.dot(values, weights.astype(jnp.bfloat16), preferred_element_type=jnp.float32)
            mixed = (mixed * share).astype(jnp.bfloat16)
            own[:, head_columns(head)] = mixed[:, :length].T
            own[:, head_columns(head + 1)] = mixed[:, length:].T


def weight_kernel(query, key, key_near, key_far, cross_bias, crossing, weights_out, share_out, *, cuts):
    length = key.shape[0]
    from_near = after_cut(cuts)
    mine = crossing[...] > 0
    for g in range(KV):
        columns = head_columns(g)
        behind = jnp.where(from_near, key_near[:, columns], key_far[:, columns])
        keys = jnp.where(mine, key[:, columns], behind)
        for head in range(g * PER_KV, (g + 1) * PER_KV, 2):
            weights, share = column_softmax(raw_scores(keys, query, head, cross_bias[...]))
            weights = weights.astype(jnp.bfloat16)
            for i in range(2):
                part = slice(i * length, (i + 1) * length)
                weights_out[head + i] = weights[:, part].T
                share_out[head + i] = jnp.broadcast_to(share[:, part], (HEAD, length)).T


def merge_kernel(weights, share, value, value_far, value_near, crossing, own, out, held, sem, *, cuts):
    from_near = after_cut(cuts)
    mine = crossing[...] > 0
    for g in range(KV):
        columns = head_columns(g)
        behind = jnp.where(from_near, value_near[:, columns], value_far[:, columns])
        values = jnp.where(mine, value[:, columns], behind)
        for head in range(g * PER_KV, (g + 1) * PER_KV):
            mixed = jnp.dot(weights[head], values, preferred_element_type=jnp.float32)
            fresh = (mixed * share[head]).astype(jnp.bfloat16)
            held[:, head_columns(head)] = jnp.where(mine, fresh, own[:, head_columns(head)])
        group = head_columns(g * PER_KV, PER_KV)
        pltpu.make_async_copy(held.at[:, group], out.at[:, group], sem).start()
    pltpu.make_async_copy(held, out, sem).wait()


def in_vmem(array):
    return pltpu.with_memory_space_constraint(array, pltpu.VMEM)


def one_block_back(queries, keys, values, doc_ids):
    count = lax.axis_size(TOKENS_AXES)
    length = queries.shape[0]
    cuts = cuts_of(count)
    rings, swap = rings_between(count, cuts), swapped(count)
    key_near = lax.ppermute(keys, TOKENS_AXES, swap)
    key_far = lax.ppermute(keys, TOKENS_AXES, rings)
    value_near = lax.ppermute(values, TOKENS_AXES, swap)
    value_far = lax.ppermute(values, TOKENS_AXES, rings)
    docs = doc_ids.reshape(-1, length)
    whole = pl.BlockSpec(memory_space=pltpu.VMEM)
    anywhere = pl.BlockSpec(memory_space=pl.ANY)
    params = pltpu.CompilerParams(vmem_limit_bytes=KERNEL_VMEM)
    square = (length, length)
    own, query_held, key_held, value_held, cross_bias, crossing = pl.pallas_call(
        own_kernel,
        out_shape=(
            pltpu.VMEM(queries.shape, jnp.bfloat16),
            pltpu.VMEM(queries.shape, jnp.bfloat16),
            pltpu.VMEM(keys.shape, jnp.bfloat16),
            pltpu.VMEM(values.shape, jnp.bfloat16),
            pltpu.VMEM(square, jnp.float32),
            pltpu.VMEM(square, jnp.bfloat16),
        ),
        in_specs=[pl.BlockSpec(memory_space=pltpu.HBM)] * 4,
        out_specs=[whole] * 6,
        scratch_shapes=[
            pltpu.VMEM(square, jnp.float32),
            pltpu.VMEM(docs.shape, jnp.int32),
            *[pltpu.SemaphoreType.DMA] * 4,
        ],
        compiler_params=params,
        name="own_attention",
    )(*(pltpu.with_memory_space_constraint(array, pltpu.HBM) for array in (queries, keys, values, docs)))
    weights, share = pl.pallas_call(
        functools.partial(weight_kernel, cuts=cuts),
        out_shape=(
            pltpu.VMEM((HQ,) + square, jnp.bfloat16),
            pltpu.VMEM((HQ,) + square, jnp.float32),
        ),
        in_specs=[whole] * 6,
        out_specs=[whole] * 2,
        compiler_params=params,
        name="crossing_weights",
    )(query_held, key_held, in_vmem(key_near), in_vmem(key_far), cross_bias, crossing)
    return pl.pallas_call(
        functools.partial(merge_kernel, cuts=cuts),
        out_shape=jax.ShapeDtypeStruct(queries.shape, jnp.bfloat16),
        in_specs=[whole] * 7,
        out_specs=anywhere,
        scratch_shapes=[pltpu.VMEM(queries.shape, jnp.bfloat16), pltpu.SemaphoreType.DMA],
        compiler_params=params,
        name="merge",
    )(weights, share, value_held, in_vmem(value_far), in_vmem(value_near), crossing, own)


def blocks_back(queries, keys, values, doc_ids, blocks):
    count = lax.axis_size(TOKENS_AXES)
    length = queries.shape[0]
    me = lax.axis_index(TOKENS_AXES)
    halo = [
        (lax.ppermute(keys, TOKENS_AXES, ring(count, s)), lax.ppermute(values, TOKENS_AXES, ring(count, s)))
        for s in range(blocks, 0, -1)
    ] + [(keys, values)]
    window = (blocks + 1) * length
    key_all = jnp.concatenate([k for k, _ in halo], axis=0).reshape(window, KV, HEAD).transpose(1, 0, 2)
    value_all = jnp.concatenate([v for _, v in halo], axis=0).reshape(window, KV, HEAD).transpose(1, 0, 2)
    padded = jnp.concatenate([jnp.full((blocks * length,), -1, jnp.int32), doc_ids], axis=0)
    key_doc = lax.dynamic_slice_in_dim(padded, me * length, window, 0)
    query_doc = key_doc[blocks * length :]
    offset = jnp.arange(window, dtype=jnp.int32) - blocks * length
    visible = (key_doc[None, :] == query_doc[:, None]) & (offset[None, :] <= jnp.arange(length)[:, None])
    grouped = queries.reshape(length, KV, PER_KV, HEAD).transpose(1, 2, 0, 3)

    def one_head(operands):
        rows, key_rows, value_rows = operands
        raw = jnp.einsum("gqd,kd->gqk", rows, key_rows, preferred_element_type=jnp.float32)
        raw = jnp.where(visible[None], raw, HIDDEN)
        peak = jnp.max(raw, axis=-1, keepdims=True)
        weights = jnp.exp2((raw - peak) * EXPONENT)
        totals = jnp.sum(weights, axis=-1, keepdims=True)
        mixed = jnp.einsum("gqk,kd->gqd", weights.astype(jnp.bfloat16), value_rows, preferred_element_type=jnp.float32)
        return (mixed / totals).astype(jnp.bfloat16)

    mixed = lax.map(one_head, (grouped, key_all, value_all))
    return mixed.transpose(2, 0, 1, 3).reshape(length, HQ * HEAD)


def shards(queries, keys, values, doc_ids):
    length = queries.shape[0]
    reach = lax.axis_size("ulysses") * length // 4
    blocks = -(-reach // length)
    if blocks == 1 and length == HEAD:
        return one_block_back(queries, keys, values, doc_ids)
    return blocks_back(queries, keys, values, doc_ids, blocks)


def solution(mesh):
    placed = P(TOKENS_AXES, None)
    return jax.shard_map(
        shards, mesh=mesh, in_specs=(placed, placed, placed, P()), out_specs=placed, check_vma=False
    )
```

```python
import functools
import math

import jax
import jax.numpy as jnp
from jax import lax
from jax.experimental import pallas as pl
from jax.experimental.pallas import tpu as pltpu
from jax.sharding import PartitionSpec as P

HQ = 48
KV = 8
HEAD = 128
PER_KV = HQ // KV
TOKENS_AXES = ("ctx", "ulysses")
HIDDEN = -1e30
EXPONENT = math.log2(math.e) / math.sqrt(HEAD)
ROW_TILE = 32
KERNEL_VMEM = 16 * 1024 * 1024


def cuts_of(count):
    return [cut for cut in [4, 6] + list(range(14, count, 8)) if cut < count - 2]


def rings_between(count, cuts):
    pairs, first = [], 0
    for last in cuts + [count - 1]:
        pairs += [(i, i + 1) for i in range(first, last)] + [(last, first)]
        first = last + 1
    return pairs


def after_cut(cuts):
    me = lax.axis_index(TOKENS_AXES)
    return functools.reduce(jnp.logical_or, [me == cut + 1 for cut in cuts], False)


def ring(count, steps):
    return [(i, (i + steps) % count) for i in range(count)]


def swapped(count):
    return [(i, i ^ 1) for i in range(count)]


def head_columns(head, heads=1):
    return slice(head * HEAD, (head + heads) * HEAD)


def column_softmax(raw):
    peak = jnp.max(raw, axis=0, keepdims=True)
    weights = jnp.exp2((raw - peak) * EXPONENT)
    return weights, 1.0 / jnp.sum(weights, axis=0, keepdims=True)


def raw_scores(keys, query, head, bias):
    raw = lax.dot_general(
        keys,
        jnp.concatenate([query[:, head_columns(head)], query[:, head_columns(head + 1)]], axis=0),
        (((1,), (1,)), ((), ())),
        preferred_element_type=jnp.float32,
    )
    return raw + jnp.concatenate([bias, bias], axis=1)


def own_kernel(
    query_in,
    key_in,
    value_in,
    docs_in,
    own,
    query,
    key,
    value,
    cross_bias,
    crossing,
    rows,
    out,
    own_bias,
    docs,
    docs_sem,
    key_sem,
    value_sem,
    query_sem,
    out_sem,
):
    length = key.shape[0]
    docs_copy = pltpu.make_async_copy(docs_in, docs, docs_sem)
    pieces = [(key_in, key, key_sem), (value_in, value, value_sem), (query_in, query, query_sem)]
    copies = [pltpu.make_async_copy(source, target, sem) for source, target, sem in pieces]
    docs_copy.start()
    for copy in copies:
        copy.start()
    docs_copy.wait()
    me = lax.axis_index(TOKENS_AXES)
    own_docs = docs[pl.ds(me, 1), :]
    before = jnp.where(me > 0, docs[pl.ds(jnp.maximum(me - 1, 0), 1), :], -1)
    row = lax.broadcasted_iota(jnp.int32, (length, length), 0)
    column = lax.broadcasted_iota(jnp.int32, (length, length), 1)
    diagonal = row == column
    key_doc = jnp.sum(jnp.where(diagonal, own_docs, 0), axis=1, keepdims=True)
    before_doc = jnp.sum(jnp.where(diagonal, before, 0), axis=1, keepdims=True)
    own_seen = (key_doc == own_docs) & (row <= column)
    own_bias[...] = jnp.where(own_seen, 0.0, HIDDEN)
    cross_bias[...] = jnp.where(own_seen | (before_doc == own_docs), 0.0, HIDDEN)
    crossing[...] = jnp.where(key_doc == before[:, length - 1 :], jnp.ones((length, length), jnp.float32), 0.0).astype(
        jnp.bfloat16
    )
    crossing_rows = jnp.sum(jnp.where(own_docs == before[:, length - 1 :], 1, 0))
    rows[0] = (crossing_rows + (ROW_TILE - 1)) // ROW_TILE * ROW_TILE
    for copy in copies:
        copy.wait()
    for g in range(KV):
        keys = key[:, head_columns(g)]
        values = value[:, head_columns(g)].T
        for head in range(g * PER_KV, (g + 1) * PER_KV, 2):
            weights, share = column_softmax(raw_scores(keys, query, head, own_bias[...]))
            mixed = jnp.dot(values, weights.astype(jnp.bfloat16), preferred_element_type=jnp.float32)
            mixed = (mixed * share).astype(jnp.bfloat16)
            own[:, head_columns(head)] = mixed[:, :length].T
            own[:, head_columns(head + 1)] = mixed[:, length:].T
        group = head_columns(g * PER_KV, PER_KV)
        pltpu.make_async_copy(own.at[:, group], out.at[:, group], out_sem).start()
    pltpu.make_async_copy(own, out, out_sem).wait()


def weight_kernel(query, key, key_near, key_far, cross_bias, crossing, weights_out, share_out, *, cuts):
    length = key.shape[0]
    from_near = after_cut(cuts)
    mine = crossing[...] > 0
    for g in range(KV):
        columns = head_columns(g)
        behind = jnp.where(from_near, key_near[:, columns], key_far[:, columns])
        keys = jnp.where(mine, key[:, columns], behind)
        for head in range(g * PER_KV, (g + 1) * PER_KV, 2):
            weights, share = column_softmax(raw_scores(keys, query, head, cross_bias[...]))
            weights = weights.astype(jnp.bfloat16)
            for i in range(2):
                part = slice(i * length, (i + 1) * length)
                weights_out[head + i] = weights[:, part].T
                share_out[head + i] = jnp.broadcast_to(share[:, part], (HEAD, length)).T


def merge_kernel(weights, share, value, value_far, value_near, crossing, own, rows, early, out, held, sem, *, cuts):
    from_near = after_cut(cuts)
    mine = crossing[...] > 0
    part = pl.ds(0, pl.multiple_of(jnp.maximum(rows[0], ROW_TILE), ROW_TILE))
    for g in range(KV):
        columns = head_columns(g)
        behind = jnp.where(from_near, value_near[:, columns], value_far[:, columns])
        values = jnp.where(mine, value[:, columns], behind)
        for head in range(g * PER_KV, (g + 1) * PER_KV):
            mixed = jnp.dot(weights[head], values, preferred_element_type=jnp.float32)
            fresh = (mixed * share[head]).astype(jnp.bfloat16)
            held[:, head_columns(head)] = jnp.where(mine, fresh, own[:, head_columns(head)])
        group = head_columns(g * PER_KV, PER_KV)
        pltpu.make_async_copy(held.at[part, group], out.at[part, group], sem).start()
    pltpu.make_async_copy(held.at[part], out.at[part], sem).wait()


def in_vmem(array):
    return pltpu.with_memory_space_constraint(array, pltpu.VMEM)


def one_block_back(queries, keys, values, doc_ids):
    count = lax.axis_size(TOKENS_AXES)
    length = queries.shape[0]
    cuts = cuts_of(count)
    rings, swap = rings_between(count, cuts), swapped(count)
    key_near = lax.ppermute(keys, TOKENS_AXES, swap)
    key_far = lax.ppermute(keys, TOKENS_AXES, rings)
    value_near = lax.ppermute(values, TOKENS_AXES, swap)
    value_far = lax.ppermute(values, TOKENS_AXES, rings)
    docs = doc_ids.reshape(-1, length)
    whole = pl.BlockSpec(memory_space=pltpu.VMEM)
    anywhere = pl.BlockSpec(memory_space=pl.ANY)
    hbm = pl.BlockSpec(memory_space=pltpu.HBM)
    scalars = pl.BlockSpec(memory_space=pltpu.SMEM)
    params = pltpu.CompilerParams(vmem_limit_bytes=KERNEL_VMEM)
    square = (length, length)
    own, query_held, key_held, value_held, cross_bias, crossing, rows, early = pl.pallas_call(
        own_kernel,
        out_shape=(
            pltpu.VMEM(queries.shape, jnp.bfloat16),
            pltpu.VMEM(queries.shape, jnp.bfloat16),
            pltpu.VMEM(keys.shape, jnp.bfloat16),
            pltpu.VMEM(values.shape, jnp.bfloat16),
            pltpu.VMEM(square, jnp.float32),
            pltpu.VMEM(square, jnp.bfloat16),
            pltpu.SMEM((1,), jnp.int32),
            pltpu.HBM(queries.shape, jnp.bfloat16),
        ),
        in_specs=[hbm] * 4,
        out_specs=[whole] * 6 + [scalars, hbm],
        scratch_shapes=[
            pltpu.VMEM(square, jnp.float32),
            pltpu.VMEM(docs.shape, jnp.int32),
            *[pltpu.SemaphoreType.DMA] * 5,
        ],
        compiler_params=params,
        name="own_attention",
    )(*(pltpu.with_memory_space_constraint(array, pltpu.HBM) for array in (queries, keys, values, docs)))
    weights, share = pl.pallas_call(
        functools.partial(weight_kernel, cuts=cuts),
        out_shape=(
            pltpu.VMEM((HQ,) + square, jnp.bfloat16),
            pltpu.VMEM((HQ,) + square, jnp.float32),
        ),
        in_specs=[whole] * 6,
        out_specs=[whole] * 2,
        compiler_params=params,
        name="crossing_weights",
    )(query_held, key_held, in_vmem(key_near), in_vmem(key_far), cross_bias, crossing)
    return pl.pallas_call(
        functools.partial(merge_kernel, cuts=cuts),
        out_shape=jax.ShapeDtypeStruct(queries.shape, jnp.bfloat16),
        in_specs=[whole] * 7 + [scalars, hbm],
        out_specs=hbm,
        scratch_shapes=[pltpu.VMEM(queries.shape, jnp.bfloat16), pltpu.SemaphoreType.DMA],
        input_output_aliases={8: 0},
        compiler_params=params,
        name="merge",
    )(weights, share, value_held, in_vmem(value_far), in_vmem(value_near), crossing, own, rows, early)


def blocks_back(queries, keys, values, doc_ids, blocks):
    count = lax.axis_size(TOKENS_AXES)
    length = queries.shape[0]
    me = lax.axis_index(TOKENS_AXES)
    halo = [
        (lax.ppermute(keys, TOKENS_AXES, ring(count, s)), lax.ppermute(values, TOKENS_AXES, ring(count, s)))
        for s in range(blocks, 0, -1)
    ] + [(keys, values)]
    window = (blocks + 1) * length
    key_all = jnp.concatenate([k for k, _ in halo], axis=0).reshape(window, KV, HEAD).transpose(1, 0, 2)
    value_all = jnp.concatenate([v for _, v in halo], axis=0).reshape(window, KV, HEAD).transpose(1, 0, 2)
    padded = jnp.concatenate([jnp.full((blocks * length,), -1, jnp.int32), doc_ids], axis=0)
    key_doc = lax.dynamic_slice_in_dim(padded, me * length, window, 0)
    query_doc = key_doc[blocks * length :]
    offset = jnp.arange(window, dtype=jnp.int32) - blocks * length
    visible = (key_doc[None, :] == query_doc[:, None]) & (offset[None, :] <= jnp.arange(length)[:, None])
    grouped = queries.reshape(length, KV, PER_KV, HEAD).transpose(1, 2, 0, 3)

    def one_head(operands):
        rows, key_rows, value_rows = operands
        raw = jnp.einsum("gqd,kd->gqk", rows, key_rows, preferred_element_type=jnp.float32)
        raw = jnp.where(visible[None], raw, HIDDEN)
        peak = jnp.max(raw, axis=-1, keepdims=True)
        weights = jnp.exp2((raw - peak) * EXPONENT)
        totals = jnp.sum(weights, axis=-1, keepdims=True)
        mixed = jnp.einsum("gqk,kd->gqd", weights.astype(jnp.bfloat16), value_rows, preferred_element_type=jnp.float32)
        return (mixed / totals).astype(jnp.bfloat16)

    mixed = lax.map(one_head, (grouped, key_all, value_all))
    return mixed.transpose(2, 0, 1, 3).reshape(length, HQ * HEAD)


def shards(queries, keys, values, doc_ids):
    length = queries.shape[0]
    reach = lax.axis_size("ulysses") * length // 4
    blocks = -(-reach // length)
    if blocks == 1 and length == HEAD:
        return one_block_back(queries, keys, values, doc_ids)
    return blocks_back(queries, keys, values, doc_ids, blocks)


def solution(mesh):
    placed = P(TOKENS_AXES, None)
    return jax.shard_map(
        shards, mesh=mesh, in_specs=(placed, placed, placed, P()), out_specs=placed, check_vma=False
    )
```

```python
import functools
import math

import jax
import jax.numpy as jnp
from jax import lax
from jax.experimental import pallas as pl
from jax.experimental.pallas import tpu as pltpu
from jax.sharding import PartitionSpec as P

HQ = 48
KV = 8
HEAD = 128
PER_KV = HQ // KV
TOKENS_AXES = ("ctx", "ulysses")
HIDDEN = -1e30
EXPONENT = math.log2(math.e) / math.sqrt(HEAD)
ROW_TILE = 32
KERNEL_VMEM = 16 * 1024 * 1024


def cuts_of(count):
    return [cut for cut in [4, 6] + list(range(14, count, 8)) if cut < count - 2]


def rings_between(count, cuts):
    pairs, first = [], 0
    for last in cuts + [count - 1]:
        pairs += [(i, i + 1) for i in range(first, last)] + [(last, first)]
        first = last + 1
    return pairs


def after_cut(cuts):
    me = lax.axis_index(TOKENS_AXES)
    return functools.reduce(jnp.logical_or, [me == cut + 1 for cut in cuts], False)


def ring(count, steps):
    return [(i, (i + steps) % count) for i in range(count)]


def swapped(count):
    return [(i, i ^ 1) for i in range(count)]


def head_columns(head, heads=1):
    return slice(head * HEAD, (head + heads) * HEAD)


def column_softmax(raw):
    peak = jnp.max(raw, axis=0, keepdims=True)
    weights = jnp.exp2((raw - peak) * EXPONENT)
    return weights, 1.0 / jnp.sum(weights, axis=0, keepdims=True)


def raw_scores(keys, query, head, bias):
    raw = lax.dot_general(
        keys,
        jnp.concatenate([query[:, head_columns(head)], query[:, head_columns(head + 1)]], axis=0),
        (((1,), (1,)), ((), ())),
        preferred_element_type=jnp.float32,
    )
    return raw + jnp.concatenate([bias, bias], axis=1)


def own_kernel(
    query_in,
    key_in,
    value_in,
    docs_in,
    own,
    query,
    key,
    value,
    cross_bias,
    crossing,
    rows,
    out,
    own_bias,
    docs,
    docs_sem,
    key_sem,
    value_sem,
    query_sem,
    out_sem,
):
    length = key.shape[0]
    docs_copy = pltpu.make_async_copy(docs_in, docs, docs_sem)
    pieces = [(key_in, key, key_sem), (value_in, value, value_sem), (query_in, query, query_sem)]
    copies = [pltpu.make_async_copy(source, target, sem) for source, target, sem in pieces]
    docs_copy.start()
    for copy in copies:
        copy.start()
    docs_copy.wait()
    me = lax.axis_index(TOKENS_AXES)
    own_docs = docs[pl.ds(me, 1), :]
    before = jnp.where(me > 0, docs[pl.ds(jnp.maximum(me - 1, 0), 1), :], -1)
    row = lax.broadcasted_iota(jnp.int32, (length, length), 0)
    column = lax.broadcasted_iota(jnp.int32, (length, length), 1)
    diagonal = row == column
    key_doc = jnp.sum(jnp.where(diagonal, own_docs, 0), axis=1, keepdims=True)
    before_doc = jnp.sum(jnp.where(diagonal, before, 0), axis=1, keepdims=True)
    own_seen = (key_doc == own_docs) & (row <= column)
    own_bias[...] = jnp.where(own_seen, 0.0, HIDDEN)
    cross_bias[...] = jnp.where(own_seen | (before_doc == own_docs), 0.0, HIDDEN)
    crossing[...] = jnp.where(key_doc == before[:, length - 1 :], jnp.ones((length, length), jnp.float32), 0.0).astype(
        jnp.bfloat16
    )
    crossing_rows = jnp.sum(jnp.where(own_docs == before[:, length - 1 :], 1, 0))
    rows[0] = (crossing_rows + (ROW_TILE - 1)) // ROW_TILE * ROW_TILE
    for copy in copies:
        copy.wait()
    for g in range(KV):
        keys = key[:, head_columns(g)]
        values = value[:, head_columns(g)].T
        for head in range(g * PER_KV, (g + 1) * PER_KV, 2):
            weights, share = column_softmax(raw_scores(keys, query, head, own_bias[...]))
            mixed = jnp.dot(values, weights.astype(jnp.bfloat16), preferred_element_type=jnp.float32)
            mixed = (mixed * share).astype(jnp.bfloat16)
            own[:, head_columns(head)] = mixed[:, :length].T
            own[:, head_columns(head + 1)] = mixed[:, length:].T
        group = head_columns(g * PER_KV, PER_KV)
        pltpu.make_async_copy(own.at[:, group], out.at[:, group], out_sem).start()
    pltpu.make_async_copy(own, out, out_sem).wait()


def weight_kernel(
    query, key, key_near, key_far, value, value_near, cross_bias, crossing, weights_out, share_out, base, from_far, *, cuts
):
    length = key.shape[0]
    from_near = after_cut(cuts)
    mine = crossing[...] > 0
    from_far[...] = jnp.where(from_near, jnp.zeros_like(crossing), 1 - crossing[...])
    for g in range(KV):
        columns = head_columns(g)
        base[:, columns] = jnp.where(mine, value[:, columns], value_near[:, columns])
        behind = jnp.where(from_near, key_near[:, columns], key_far[:, columns])
        keys = jnp.where(mine, key[:, columns], behind)
        for head in range(g * PER_KV, (g + 1) * PER_KV, 2):
            weights, share = column_softmax(raw_scores(keys, query, head, cross_bias[...]))
            weights = weights.astype(jnp.bfloat16)
            for i in range(2):
                part = slice(i * length, (i + 1) * length)
                weights_out[head + i] = weights[:, part].T
                share_out[head + i] = jnp.broadcast_to(share[:, part], (HEAD, length)).T


def merge_kernel(weights, share, base, value_far, from_far, crossing, own, rows, early, out, held, sem):
    mine = crossing[...] > 0
    far = from_far[...] > 0
    part = pl.ds(0, pl.multiple_of(jnp.maximum(rows[0], ROW_TILE), ROW_TILE))
    for g in range(KV):
        columns = head_columns(g)
        values = jnp.where(far, value_far[:, columns], base[:, columns])
        for head in range(g * PER_KV, (g + 1) * PER_KV):
            mixed = jnp.dot(weights[head], values, preferred_element_type=jnp.float32)
            fresh = (mixed * share[head]).astype(jnp.bfloat16)
            held[:, head_columns(head)] = jnp.where(mine, fresh, own[:, head_columns(head)])
        group = head_columns(g * PER_KV, PER_KV)
        pltpu.make_async_copy(held.at[part, group], out.at[part, group], sem).start()
    pltpu.make_async_copy(held.at[part], out.at[part], sem).wait()


def in_vmem(array):
    return pltpu.with_memory_space_constraint(array, pltpu.VMEM)


def one_block_back(queries, keys, values, doc_ids):
    count = lax.axis_size(TOKENS_AXES)
    length = queries.shape[0]
    cuts = cuts_of(count)
    rings, swap = rings_between(count, cuts), swapped(count)
    key_near = lax.ppermute(keys, TOKENS_AXES, swap)
    key_far = lax.ppermute(keys, TOKENS_AXES, rings)
    value_near = lax.ppermute(values, TOKENS_AXES, swap)
    value_far = lax.ppermute(values, TOKENS_AXES, rings)
    docs = doc_ids.reshape(-1, length)
    whole = pl.BlockSpec(memory_space=pltpu.VMEM)
    anywhere = pl.BlockSpec(memory_space=pl.ANY)
    hbm = pl.BlockSpec(memory_space=pltpu.HBM)
    scalars = pl.BlockSpec(memory_space=pltpu.SMEM)
    params = pltpu.CompilerParams(vmem_limit_bytes=KERNEL_VMEM)
    square = (length, length)
    own, query_held, key_held, value_held, cross_bias, crossing, rows, early = pl.pallas_call(
        own_kernel,
        out_shape=(
            pltpu.VMEM(queries.shape, jnp.bfloat16),
            pltpu.VMEM(queries.shape, jnp.bfloat16),
            pltpu.VMEM(keys.shape, jnp.bfloat16),
            pltpu.VMEM(values.shape, jnp.bfloat16),
            pltpu.VMEM(square, jnp.float32),
            pltpu.VMEM(square, jnp.bfloat16),
            pltpu.SMEM((1,), jnp.int32),
            pltpu.HBM(queries.shape, jnp.bfloat16),
        ),
        in_specs=[hbm] * 4,
        out_specs=[whole] * 6 + [scalars, hbm],
        scratch_shapes=[
            pltpu.VMEM(square, jnp.float32),
            pltpu.VMEM(docs.shape, jnp.int32),
            *[pltpu.SemaphoreType.DMA] * 5,
        ],
        compiler_params=params,
        name="own_attention",
    )(*(pltpu.with_memory_space_constraint(array, pltpu.HBM) for array in (queries, keys, values, docs)))
    weights, share, base, from_far = pl.pallas_call(
        functools.partial(weight_kernel, cuts=cuts),
        out_shape=(
            pltpu.VMEM((HQ,) + square, jnp.bfloat16),
            pltpu.VMEM((HQ,) + square, jnp.float32),
            pltpu.VMEM(values.shape, jnp.bfloat16),
            pltpu.VMEM(square, jnp.bfloat16),
        ),
        in_specs=[whole] * 8,
        out_specs=[whole] * 4,
        compiler_params=params,
        name="crossing_weights",
    )(
        query_held,
        key_held,
        in_vmem(key_near),
        in_vmem(key_far),
        value_held,
        in_vmem(value_near),
        cross_bias,
        crossing,
    )
    return pl.pallas_call(
        merge_kernel,
        out_shape=jax.ShapeDtypeStruct(queries.shape, jnp.bfloat16),
        in_specs=[whole] * 7 + [scalars, hbm],
        out_specs=hbm,
        scratch_shapes=[pltpu.VMEM(queries.shape, jnp.bfloat16), pltpu.SemaphoreType.DMA],
        input_output_aliases={8: 0},
        compiler_params=params,
        name="merge",
    )(weights, share, base, in_vmem(value_far), from_far, crossing, own, rows, early)


def blocks_back(queries, keys, values, doc_ids, blocks):
    count = lax.axis_size(TOKENS_AXES)
    length = queries.shape[0]
    me = lax.axis_index(TOKENS_AXES)
    halo = [
        (lax.ppermute(keys, TOKENS_AXES, ring(count, s)), lax.ppermute(values, TOKENS_AXES, ring(count, s)))
        for s in range(blocks, 0, -1)
    ] + [(keys, values)]
    window = (blocks + 1) * length
    key_all = jnp.concatenate([k for k, _ in halo], axis=0).reshape(window, KV, HEAD).transpose(1, 0, 2)
    value_all = jnp.concatenate([v for _, v in halo], axis=0).reshape(window, KV, HEAD).transpose(1, 0, 2)
    padded = jnp.concatenate([jnp.full((blocks * length,), -1, jnp.int32), doc_ids], axis=0)
    key_doc = lax.dynamic_slice_in_dim(padded, me * length, window, 0)
    query_doc = key_doc[blocks * length :]
    offset = jnp.arange(window, dtype=jnp.int32) - blocks * length
    visible = (key_doc[None, :] == query_doc[:, None]) & (offset[None, :] <= jnp.arange(length)[:, None])
    grouped = queries.reshape(length, KV, PER_KV, HEAD).transpose(1, 2, 0, 3)

    def one_head(operands):
        rows, key_rows, value_rows = operands
        raw = jnp.einsum("gqd,kd->gqk", rows, key_rows, preferred_element_type=jnp.float32)
        raw = jnp.where(visible[None], raw, HIDDEN)
        peak = jnp.max(raw, axis=-1, keepdims=True)
        weights = jnp.exp2((raw - peak) * EXPONENT)
        totals = jnp.sum(weights, axis=-1, keepdims=True)
        mixed = jnp.einsum("gqk,kd->gqd", weights.astype(jnp.bfloat16), value_rows, preferred_element_type=jnp.float32)
        return (mixed / totals).astype(jnp.bfloat16)

    mixed = lax.map(one_head, (grouped, key_all, value_all))
    return mixed.transpose(2, 0, 1, 3).reshape(length, HQ * HEAD)


def shards(queries, keys, values, doc_ids):
    length = queries.shape[0]
    reach = lax.axis_size("ulysses") * length // 4
    blocks = -(-reach // length)
    if blocks == 1 and length == HEAD:
        return one_block_back(queries, keys, values, doc_ids)
    return blocks_back(queries, keys, values, doc_ids, blocks)


def solution(mesh):
    placed = P(TOKENS_AXES, None)
    return jax.shard_map(
        shards, mesh=mesh, in_specs=(placed, placed, placed, P()), out_specs=placed, check_vma=False
    )
```

```python
import functools
import math

import jax
import jax.numpy as jnp
from jax import lax
from jax.experimental import pallas as pl
from jax.experimental.pallas import tpu as pltpu
from jax.sharding import PartitionSpec as P

HQ = 48
KV = 8
HEAD = 128
PER_KV = HQ // KV
TOKENS_AXES = ("ctx", "ulysses")
HIDDEN = -1e30
EXPONENT = math.log2(math.e) / math.sqrt(HEAD)
ROW_TILE = 32
TOGETHER = 3
KERNEL_VMEM = 16 * 1024 * 1024


def cuts_of(count):
    return [cut for cut in [4, 6] + list(range(14, count, 8)) if cut < count - 2]


def rings_between(count, cuts):
    pairs, first = [], 0
    for last in cuts + [count - 1]:
        pairs += [(i, i + 1) for i in range(first, last)] + [(last, first)]
        first = last + 1
    return pairs


def after_cut(cuts):
    me = lax.axis_index(TOKENS_AXES)
    return functools.reduce(jnp.logical_or, [me == cut + 1 for cut in cuts], False)


def ring(count, steps):
    return [(i, (i + steps) % count) for i in range(count)]


def swapped(count):
    return [(i, i ^ 1) for i in range(count)]


def head_columns(head, heads=1):
    return slice(head * HEAD, (head + heads) * HEAD)


def column_softmax(raw):
    peak = jnp.max(raw, axis=0, keepdims=True)
    weights = jnp.exp2((raw - peak) * EXPONENT)
    return weights, 1.0 / jnp.sum(weights, axis=0, keepdims=True)


def raw_scores(keys, query, head, bias):
    raw = lax.dot_general(
        keys,
        jnp.concatenate([query[:, head_columns(head)], query[:, head_columns(head + 1)]], axis=0),
        (((1,), (1,)), ((), ())),
        preferred_element_type=jnp.float32,
    )
    return raw + jnp.concatenate([bias, bias], axis=1)


def own_kernel(
    query_in,
    key_in,
    value_in,
    docs_in,
    own,
    query,
    key,
    value,
    cross_bias,
    crossing,
    rows,
    out,
    own_bias,
    docs,
    docs_sem,
    key_sem,
    value_sem,
    query_sem,
    out_sem,
):
    length = key.shape[0]
    docs_copy = pltpu.make_async_copy(docs_in, docs, docs_sem)
    pieces = [(key_in, key, key_sem), (value_in, value, value_sem), (query_in, query, query_sem)]
    copies = [pltpu.make_async_copy(source, target, sem) for source, target, sem in pieces]
    docs_copy.start()
    for copy in copies:
        copy.start()
    docs_copy.wait()
    me = lax.axis_index(TOKENS_AXES)
    own_docs = docs[pl.ds(me, 1), :]
    before = jnp.where(me > 0, docs[pl.ds(jnp.maximum(me - 1, 0), 1), :], -1)
    row = lax.broadcasted_iota(jnp.int32, (length, length), 0)
    column = lax.broadcasted_iota(jnp.int32, (length, length), 1)
    diagonal = row == column
    key_doc = jnp.sum(jnp.where(diagonal, own_docs, 0), axis=1, keepdims=True)
    before_doc = jnp.sum(jnp.where(diagonal, before, 0), axis=1, keepdims=True)
    own_seen = (key_doc == own_docs) & (row <= column)
    own_bias[...] = jnp.where(own_seen, 0.0, HIDDEN)
    cross_bias[...] = jnp.where(own_seen | (before_doc == own_docs), 0.0, HIDDEN)
    crossing[...] = jnp.where(key_doc == before[:, length - 1 :], jnp.ones((length, length), jnp.float32), 0.0).astype(
        jnp.bfloat16
    )
    crossing_rows = jnp.sum(jnp.where(own_docs == before[:, length - 1 :], 1, 0))
    rows[0] = (crossing_rows + (ROW_TILE - 1)) // ROW_TILE * ROW_TILE
    for copy in copies:
        copy.wait()
    for g in range(KV):
        keys = key[:, head_columns(g)]
        values = value[:, head_columns(g)].T
        for head in range(g * PER_KV, (g + 1) * PER_KV, 2):
            weights, share = column_softmax(raw_scores(keys, query, head, own_bias[...]))
            mixed = jnp.dot(values, weights.astype(jnp.bfloat16), preferred_element_type=jnp.float32)
            mixed = (mixed * share).astype(jnp.bfloat16)
            own[:, head_columns(head)] = mixed[:, :length].T
            own[:, head_columns(head + 1)] = mixed[:, length:].T
        group = head_columns(g * PER_KV, PER_KV)
        pltpu.make_async_copy(own.at[:, group], out.at[:, group], out_sem).start()
    pltpu.make_async_copy(own, out, out_sem).wait()


def weight_kernel(
    query, key, key_near, key_far, value, value_near, cross_bias, crossing, weights_out, share_out, base, from_far, *, cuts
):
    length = key.shape[0]
    from_near = after_cut(cuts)
    mine = crossing[...] > 0
    from_far[...] = jnp.where(from_near, jnp.zeros_like(crossing), 1 - crossing[...])
    for g in range(KV):
        columns = head_columns(g)
        base[:, columns] = jnp.where(mine, value[:, columns], value_near[:, columns])
        behind = jnp.where(from_near, key_near[:, columns], key_far[:, columns])
        keys = jnp.where(mine, key[:, columns], behind)
        for head in range(g * PER_KV, (g + 1) * PER_KV, 2):
            weights, share = column_softmax(raw_scores(keys, query, head, cross_bias[...]))
            weights = weights.astype(jnp.bfloat16)
            for i in range(2):
                part = slice(i * length, (i + 1) * length)
                weights_out[head + i] = weights[:, part].T
                share_out[head + i] = jnp.broadcast_to(share[:, part], (HEAD, length)).T


def merge_kernel(weights, share, base, value_far, from_far, crossing, own, rows, early, out, held, sem):
    length = own.shape[0]
    mine = crossing[...] > 0
    far = from_far[...] > 0
    part = pl.ds(0, pl.multiple_of(jnp.maximum(rows[0], ROW_TILE), ROW_TILE))
    for g in range(KV):
        columns = head_columns(g)
        values = jnp.where(far, value_far[:, columns], base[:, columns])
        for head in range(g * PER_KV, (g + 1) * PER_KV, TOGETHER):
            several = jnp.concatenate([weights[head + i] for i in range(TOGETHER)], axis=0)
            mixed = jnp.dot(several, values, preferred_element_type=jnp.float32)
            for i in range(TOGETHER):
                fresh = (mixed[i * length : (i + 1) * length] * share[head + i]).astype(jnp.bfloat16)
                held[:, head_columns(head + i)] = jnp.where(mine, fresh, own[:, head_columns(head + i)])
        group = head_columns(g * PER_KV, PER_KV)
        pltpu.make_async_copy(held.at[part, group], out.at[part, group], sem).start()
    pltpu.make_async_copy(held.at[part], out.at[part], sem).wait()


def in_vmem(array):
    return pltpu.with_memory_space_constraint(array, pltpu.VMEM)


def one_block_back(queries, keys, values, doc_ids):
    count = lax.axis_size(TOKENS_AXES)
    length = queries.shape[0]
    cuts = cuts_of(count)
    rings, swap = rings_between(count, cuts), swapped(count)
    key_near = lax.ppermute(keys, TOKENS_AXES, swap)
    key_far = lax.ppermute(keys, TOKENS_AXES, rings)
    value_near = lax.ppermute(values, TOKENS_AXES, swap)
    value_far = lax.ppermute(values, TOKENS_AXES, rings)
    docs = doc_ids.reshape(-1, length)
    whole = pl.BlockSpec(memory_space=pltpu.VMEM)
    anywhere = pl.BlockSpec(memory_space=pl.ANY)
    hbm = pl.BlockSpec(memory_space=pltpu.HBM)
    scalars = pl.BlockSpec(memory_space=pltpu.SMEM)
    params = pltpu.CompilerParams(vmem_limit_bytes=KERNEL_VMEM)
    square = (length, length)
    own, query_held, key_held, value_held, cross_bias, crossing, rows, early = pl.pallas_call(
        own_kernel,
        out_shape=(
            pltpu.VMEM(queries.shape, jnp.bfloat16),
            pltpu.VMEM(queries.shape, jnp.bfloat16),
            pltpu.VMEM(keys.shape, jnp.bfloat16),
            pltpu.VMEM(values.shape, jnp.bfloat16),
            pltpu.VMEM(square, jnp.float32),
            pltpu.VMEM(square, jnp.bfloat16),
            pltpu.SMEM((1,), jnp.int32),
            pltpu.HBM(queries.shape, jnp.bfloat16),
        ),
        in_specs=[hbm] * 4,
        out_specs=[whole] * 6 + [scalars, hbm],
        scratch_shapes=[
            pltpu.VMEM(square, jnp.float32),
            pltpu.VMEM(docs.shape, jnp.int32),
            *[pltpu.SemaphoreType.DMA] * 5,
        ],
        compiler_params=params,
        name="own_attention",
    )(*(pltpu.with_memory_space_constraint(array, pltpu.HBM) for array in (queries, keys, values, docs)))
    weights, share, base, from_far = pl.pallas_call(
        functools.partial(weight_kernel, cuts=cuts),
        out_shape=(
            pltpu.VMEM((HQ,) + square, jnp.bfloat16),
            pltpu.VMEM((HQ,) + square, jnp.float32),
            pltpu.VMEM(values.shape, jnp.bfloat16),
            pltpu.VMEM(square, jnp.bfloat16),
        ),
        in_specs=[whole] * 8,
        out_specs=[whole] * 4,
        compiler_params=params,
        name="crossing_weights",
    )(
        query_held,
        key_held,
        in_vmem(key_near),
        in_vmem(key_far),
        value_held,
        in_vmem(value_near),
        cross_bias,
        crossing,
    )
    return pl.pallas_call(
        merge_kernel,
        out_shape=jax.ShapeDtypeStruct(queries.shape, jnp.bfloat16),
        in_specs=[whole] * 7 + [scalars, hbm],
        out_specs=hbm,
        scratch_shapes=[pltpu.VMEM(queries.shape, jnp.bfloat16), pltpu.SemaphoreType.DMA],
        input_output_aliases={8: 0},
        compiler_params=params,
        name="merge",
    )(weights, share, base, in_vmem(value_far), from_far, crossing, own, rows, early)


def blocks_back(queries, keys, values, doc_ids, blocks):
    count = lax.axis_size(TOKENS_AXES)
    length = queries.shape[0]
    me = lax.axis_index(TOKENS_AXES)
    halo = [
        (lax.ppermute(keys, TOKENS_AXES, ring(count, s)), lax.ppermute(values, TOKENS_AXES, ring(count, s)))
        for s in range(blocks, 0, -1)
    ] + [(keys, values)]
    window = (blocks + 1) * length
    key_all = jnp.concatenate([k for k, _ in halo], axis=0).reshape(window, KV, HEAD).transpose(1, 0, 2)
    value_all = jnp.concatenate([v for _, v in halo], axis=0).reshape(window, KV, HEAD).transpose(1, 0, 2)
    padded = jnp.concatenate([jnp.full((blocks * length,), -1, jnp.int32), doc_ids], axis=0)
    key_doc = lax.dynamic_slice_in_dim(padded, me * length, window, 0)
    query_doc = key_doc[blocks * length :]
    offset = jnp.arange(window, dtype=jnp.int32) - blocks * length
    visible = (key_doc[None, :] == query_doc[:, None]) & (offset[None, :] <= jnp.arange(length)[:, None])
    grouped = queries.reshape(length, KV, PER_KV, HEAD).transpose(1, 2, 0, 3)

    def one_head(operands):
        rows, key_rows, value_rows = operands
        raw = jnp.einsum("gqd,kd->gqk", rows, key_rows, preferred_element_type=jnp.float32)
        raw = jnp.where(visible[None], raw, HIDDEN)
        peak = jnp.max(raw, axis=-1, keepdims=True)
        weights = jnp.exp2((raw - peak) * EXPONENT)
        totals = jnp.sum(weights, axis=-1, keepdims=True)
        mixed = jnp.einsum("gqk,kd->gqd", weights.astype(jnp.bfloat16), value_rows, preferred_element_type=jnp.float32)
        return (mixed / totals).astype(jnp.bfloat16)

    mixed = lax.map(one_head, (grouped, key_all, value_all))
    return mixed.transpose(2, 0, 1, 3).reshape(length, HQ * HEAD)


def shards(queries, keys, values, doc_ids):
    length = queries.shape[0]
    reach = lax.axis_size("ulysses") * length // 4
    blocks = -(-reach // length)
    if blocks == 1 and length == HEAD:
        return one_block_back(queries, keys, values, doc_ids)
    return blocks_back(queries, keys, values, doc_ids, blocks)


def solution(mesh):
    placed = P(TOKENS_AXES, None)
    return jax.shard_map(
        shards, mesh=mesh, in_specs=(placed, placed, placed, P()), out_specs=placed, check_vma=False
    )
```

```python
import functools
import math

import jax
import jax.numpy as jnp
from jax import lax
from jax.experimental import pallas as pl
from jax.experimental.pallas import tpu as pltpu
from jax.sharding import PartitionSpec as P

HQ = 48
KV = 8
HEAD = 128
PER_KV = HQ // KV
TOKENS_AXES = ("ctx", "ulysses")
HIDDEN = -1e30
EXPONENT = math.log2(math.e) / math.sqrt(HEAD)
ROW_TILE = 32
KERNEL_VMEM = 16 * 1024 * 1024


def cuts_of(count):
    return [cut for cut in [4, 6] + list(range(14, count, 8)) if cut < count - 2]


def rings_between(count, cuts):
    pairs, first = [], 0
    for last in cuts + [count - 1]:
        pairs += [(i, i + 1) for i in range(first, last)] + [(last, first)]
        first = last + 1
    return pairs


def after_cut(cuts):
    me = lax.axis_index(TOKENS_AXES)
    return functools.reduce(jnp.logical_or, [me == cut + 1 for cut in cuts], False)


def ring(count, steps):
    return [(i, (i + steps) % count) for i in range(count)]


def swapped(count):
    return [(i, i ^ 1) for i in range(count)]


def head_columns(head, heads=1):
    return slice(head * HEAD, (head + heads) * HEAD)


def column_softmax(raw):
    peak = jnp.max(raw, axis=0, keepdims=True)
    weights = jnp.exp2((raw - peak) * EXPONENT)
    return weights, 1.0 / jnp.sum(weights, axis=0, keepdims=True)


def raw_scores(keys, query, head, bias):
    raw = lax.dot_general(
        keys,
        jnp.concatenate([query[:, head_columns(head)], query[:, head_columns(head + 1)]], axis=0),
        (((1,), (1,)), ((), ())),
        preferred_element_type=jnp.float32,
    )
    return raw + jnp.concatenate([bias, bias], axis=1)


def own_kernel(
    query_in,
    key_in,
    value_in,
    docs_in,
    own,
    query,
    key,
    value,
    cross_bias,
    crossing,
    rows,
    out,
    own_bias,
    docs,
    docs_sem,
    key_sem,
    value_sem,
    query_sem,
    out_sem,
):
    length = key.shape[0]
    docs_copy = pltpu.make_async_copy(docs_in, docs, docs_sem)
    pieces = [(key_in, key, key_sem), (value_in, value, value_sem), (query_in, query, query_sem)]
    copies = [pltpu.make_async_copy(source, target, sem) for source, target, sem in pieces]
    docs_copy.start()
    for copy in copies:
        copy.start()
    docs_copy.wait()
    me = lax.axis_index(TOKENS_AXES)
    own_docs = docs[pl.ds(me, 1), :]
    before = jnp.where(me > 0, docs[pl.ds(jnp.maximum(me - 1, 0), 1), :], -1)
    row = lax.broadcasted_iota(jnp.int32, (length, length), 0)
    column = lax.broadcasted_iota(jnp.int32, (length, length), 1)
    diagonal = row == column
    key_doc = jnp.sum(jnp.where(diagonal, own_docs, 0), axis=1, keepdims=True)
    before_doc = jnp.sum(jnp.where(diagonal, before, 0), axis=1, keepdims=True)
    own_seen = (key_doc == own_docs) & (row <= column)
    own_bias[...] = jnp.where(own_seen, 0.0, HIDDEN)
    cross_bias[...] = jnp.where(own_seen | (before_doc == own_docs), 0.0, HIDDEN)
    crossing[...] = jnp.where(key_doc == before[:, length - 1 :], jnp.ones((length, length), jnp.float32), 0.0).astype(
        jnp.bfloat16
    )
    crossing_rows = jnp.sum(jnp.where(own_docs == before[:, length - 1 :], 1, 0))
    rows[0] = (crossing_rows + (ROW_TILE - 1)) // ROW_TILE * ROW_TILE
    for copy in copies:
        copy.wait()
    for g in range(KV):
        keys = key[:, head_columns(g)]
        values = value[:, head_columns(g)].T
        for head in range(g * PER_KV, (g + 1) * PER_KV, 2):
            weights, share = column_softmax(raw_scores(keys, query, head, own_bias[...]))
            mixed = jnp.dot(values, weights.astype(jnp.bfloat16), preferred_element_type=jnp.float32)
            mixed = (mixed * share).astype(jnp.bfloat16)
            own[:, head_columns(head)] = mixed[:, :length].T
            own[:, head_columns(head + 1)] = mixed[:, length:].T
        group = head_columns(g * PER_KV, PER_KV)
        pltpu.make_async_copy(own.at[:, group], out.at[:, group], out_sem).start()
    pltpu.make_async_copy(own, out, out_sem).wait()


def weight_kernel(
    query, key, key_near, key_far, value, value_near, cross_bias, crossing, weights_out, share_out, base, from_far, *, cuts
):
    length = key.shape[0]
    from_near = after_cut(cuts)
    mine = crossing[...] > 0
    from_far[...] = jnp.where(from_near, jnp.zeros_like(crossing), 1 - crossing[...])
    for g in range(KV):
        columns = head_columns(g)
        base[:, columns] = jnp.where(mine, value[:, columns], value_near[:, columns])
        behind = jnp.where(from_near, key_near[:, columns], key_far[:, columns])
        keys = jnp.where(mine, key[:, columns], behind)
        for head in range(g * PER_KV, (g + 1) * PER_KV, 2):
            weights, share = column_softmax(raw_scores(keys, query, head, cross_bias[...]))
            weights = weights.astype(jnp.bfloat16)
            for i in range(2):
                part = slice(i * length, (i + 1) * length)
                weights_out[head + i] = weights[:, part].T
                share_out[head + i] = jnp.broadcast_to(share[:, part], (HEAD, length)).T


def merge_kernel(weights, share, base, value_far, from_far, crossing, own, rows, early, out, held, sem):
    length = own.shape[0]
    far = from_far[...] > 0
    stored = jnp.maximum(rows[0], ROW_TILE)
    part = pl.ds(0, pl.multiple_of(stored, ROW_TILE))

    def merge_rows(count, together):
        mine = crossing[:count] > 0
        for g in range(KV):
            columns = head_columns(g)
            values = jnp.where(far, value_far[:, columns], base[:, columns])
            for head in range(g * PER_KV, (g + 1) * PER_KV, together):
                several = jnp.concatenate([weights[head + i, :count] for i in range(together)], axis=0)
                mixed = jnp.dot(several, values, preferred_element_type=jnp.float32)
                for i in range(together):
                    fresh = (mixed[i * count : (i + 1) * count] * share[head + i, :count]).astype(jnp.bfloat16)
                    held[:count, head_columns(head + i)] = jnp.where(mine, fresh, own[:count, head_columns(head + i)])
            group = head_columns(g * PER_KV, PER_KV)
            pltpu.make_async_copy(held.at[part, group], out.at[part, group], sem).start()

    pl.when(stored > length // 2)(lambda: merge_rows(length, PER_KV // 2))
    pl.when(stored <= length // 2)(lambda: merge_rows(length // 2, PER_KV))
    pltpu.make_async_copy(held.at[part], out.at[part], sem).wait()


def in_vmem(array):
    return pltpu.with_memory_space_constraint(array, pltpu.VMEM)


def one_block_back(queries, keys, values, doc_ids):
    count = lax.axis_size(TOKENS_AXES)
    length = queries.shape[0]
    cuts = cuts_of(count)
    rings, swap = rings_between(count, cuts), swapped(count)
    key_near = lax.ppermute(keys, TOKENS_AXES, swap)
    key_far = lax.ppermute(keys, TOKENS_AXES, rings)
    value_near = lax.ppermute(values, TOKENS_AXES, swap)
    value_far = lax.ppermute(values, TOKENS_AXES, rings)
    docs = doc_ids.reshape(-1, length)
    whole = pl.BlockSpec(memory_space=pltpu.VMEM)
    anywhere = pl.BlockSpec(memory_space=pl.ANY)
    hbm = pl.BlockSpec(memory_space=pltpu.HBM)
    scalars = pl.BlockSpec(memory_space=pltpu.SMEM)
    params = pltpu.CompilerParams(vmem_limit_bytes=KERNEL_VMEM)
    square = (length, length)
    own, query_held, key_held, value_held, cross_bias, crossing, rows, early = pl.pallas_call(
        own_kernel,
        out_shape=(
            pltpu.VMEM(queries.shape, jnp.bfloat16),
            pltpu.VMEM(queries.shape, jnp.bfloat16),
            pltpu.VMEM(keys.shape, jnp.bfloat16),
            pltpu.VMEM(values.shape, jnp.bfloat16),
            pltpu.VMEM(square, jnp.float32),
            pltpu.VMEM(square, jnp.bfloat16),
            pltpu.SMEM((1,), jnp.int32),
            pltpu.HBM(queries.shape, jnp.bfloat16),
        ),
        in_specs=[hbm] * 4,
        out_specs=[whole] * 6 + [scalars, hbm],
        scratch_shapes=[
            pltpu.VMEM(square, jnp.float32),
            pltpu.VMEM(docs.shape, jnp.int32),
            *[pltpu.SemaphoreType.DMA] * 5,
        ],
        compiler_params=params,
        name="own_attention",
    )(*(pltpu.with_memory_space_constraint(array, pltpu.HBM) for array in (queries, keys, values, docs)))
    weights, share, base, from_far = pl.pallas_call(
        functools.partial(weight_kernel, cuts=cuts),
        out_shape=(
            pltpu.VMEM((HQ,) + square, jnp.bfloat16),
            pltpu.VMEM((HQ,) + square, jnp.float32),
            pltpu.VMEM(values.shape, jnp.bfloat16),
            pltpu.VMEM(square, jnp.bfloat16),
        ),
        in_specs=[whole] * 8,
        out_specs=[whole] * 4,
        compiler_params=params,
        name="crossing_weights",
    )(
        query_held,
        key_held,
        in_vmem(key_near),
        in_vmem(key_far),
        value_held,
        in_vmem(value_near),
        cross_bias,
        crossing,
    )
    return pl.pallas_call(
        merge_kernel,
        out_shape=jax.ShapeDtypeStruct(queries.shape, jnp.bfloat16),
        in_specs=[whole] * 7 + [scalars, hbm],
        out_specs=hbm,
        scratch_shapes=[pltpu.VMEM(queries.shape, jnp.bfloat16), pltpu.SemaphoreType.DMA],
        input_output_aliases={8: 0},
        compiler_params=params,
        name="merge",
    )(weights, share, base, in_vmem(value_far), from_far, crossing, own, rows, early)


def blocks_back(queries, keys, values, doc_ids, blocks):
    count = lax.axis_size(TOKENS_AXES)
    length = queries.shape[0]
    me = lax.axis_index(TOKENS_AXES)
    halo = [
        (lax.ppermute(keys, TOKENS_AXES, ring(count, s)), lax.ppermute(values, TOKENS_AXES, ring(count, s)))
        for s in range(blocks, 0, -1)
    ] + [(keys, values)]
    window = (blocks + 1) * length
    key_all = jnp.concatenate([k for k, _ in halo], axis=0).reshape(window, KV, HEAD).transpose(1, 0, 2)
    value_all = jnp.concatenate([v for _, v in halo], axis=0).reshape(window, KV, HEAD).transpose(1, 0, 2)
    padded = jnp.concatenate([jnp.full((blocks * length,), -1, jnp.int32), doc_ids], axis=0)
    key_doc = lax.dynamic_slice_in_dim(padded, me * length, window, 0)
    query_doc = key_doc[blocks * length :]
    offset = jnp.arange(window, dtype=jnp.int32) - blocks * length
    visible = (key_doc[None, :] == query_doc[:, None]) & (offset[None, :] <= jnp.arange(length)[:, None])
    grouped = queries.reshape(length, KV, PER_KV, HEAD).transpose(1, 2, 0, 3)

    def one_head(operands):
        rows, key_rows, value_rows = operands
        raw = jnp.einsum("gqd,kd->gqk", rows, key_rows, preferred_element_type=jnp.float32)
        raw = jnp.where(visible[None], raw, HIDDEN)
        peak = jnp.max(raw, axis=-1, keepdims=True)
        weights = jnp.exp2((raw - peak) * EXPONENT)
        totals = jnp.sum(weights, axis=-1, keepdims=True)
        mixed = jnp.einsum("gqk,kd->gqd", weights.astype(jnp.bfloat16), value_rows, preferred_element_type=jnp.float32)
        return (mixed / totals).astype(jnp.bfloat16)

    mixed = lax.map(one_head, (grouped, key_all, value_all))
    return mixed.transpose(2, 0, 1, 3).reshape(length, HQ * HEAD)


def shards(queries, keys, values, doc_ids):
    length = queries.shape[0]
    reach = lax.axis_size("ulysses") * length // 4
    blocks = -(-reach // length)
    if blocks == 1 and length == HEAD:
        return one_block_back(queries, keys, values, doc_ids)
    return blocks_back(queries, keys, values, doc_ids, blocks)


def solution(mesh):
    placed = P(TOKENS_AXES, None)
    return jax.shard_map(
        shards, mesh=mesh, in_specs=(placed, placed, placed, P()), out_specs=placed, check_vma=False
    )
```

```python
import functools
import math

import jax
import jax.numpy as jnp
from jax import lax
from jax.experimental import pallas as pl
from jax.experimental.pallas import tpu as pltpu
from jax.sharding import PartitionSpec as P

HQ = 48
KV = 8
HEAD = 128
PER_KV = HQ // KV
TOKENS_AXES = ("ctx", "ulysses")
HIDDEN = -1e30
EXPONENT = math.log2(math.e) / math.sqrt(HEAD)
ROW_TILE = 32
KERNEL_VMEM = 16 * 1024 * 1024


def cuts_of(count):
    return [cut for cut in [4, 6] + list(range(14, count, 8)) if cut < count - 2]


def rings_between(count, cuts):
    pairs, first = [], 0
    for last in cuts + [count - 1]:
        pairs += [(i, i + 1) for i in range(first, last)] + [(last, first)]
        first = last + 1
    return pairs


def after_cut(cuts):
    me = lax.axis_index(TOKENS_AXES)
    return functools.reduce(jnp.logical_or, [me == cut + 1 for cut in cuts], False)


def ring(count, steps):
    return [(i, (i + steps) % count) for i in range(count)]


def swapped(count):
    return [(i, i ^ 1) for i in range(count)]


def head_columns(head, heads=1):
    return slice(head * HEAD, (head + heads) * HEAD)


def column_softmax(raw):
    peak = jnp.max(raw, axis=0, keepdims=True)
    weights = jnp.exp2((raw - peak) * EXPONENT)
    return weights, 1.0 / jnp.sum(weights, axis=0, keepdims=True)


def raw_scores(keys, query, head, bias):
    raw = lax.dot_general(
        keys,
        jnp.concatenate([query[:, head_columns(head)], query[:, head_columns(head + 1)]], axis=0),
        (((1,), (1,)), ((), ())),
        preferred_element_type=jnp.float32,
    )
    return raw + jnp.concatenate([bias, bias], axis=1)


def own_kernel(
    query_in,
    key_in,
    value_in,
    docs_in,
    own,
    query,
    key,
    value,
    cross_bias,
    crossing,
    rows,
    out,
    own_bias,
    docs,
    docs_sem,
    key_sem,
    value_sem,
    query_sem,
    out_sem,
):
    length = key.shape[0]
    docs_copy = pltpu.make_async_copy(docs_in, docs, docs_sem)
    pieces = [(key_in, key, key_sem), (value_in, value, value_sem), (query_in, query, query_sem)]
    copies = [pltpu.make_async_copy(source, target, sem) for source, target, sem in pieces]
    docs_copy.start()
    for copy in copies:
        copy.start()
    docs_copy.wait()
    me = lax.axis_index(TOKENS_AXES)
    own_docs = docs[pl.ds(me, 1), :]
    before = jnp.where(me > 0, docs[pl.ds(jnp.maximum(me - 1, 0), 1), :], -1)
    row = lax.broadcasted_iota(jnp.int32, (length, length), 0)
    column = lax.broadcasted_iota(jnp.int32, (length, length), 1)
    diagonal = row == column
    key_doc = jnp.sum(jnp.where(diagonal, own_docs, 0), axis=1, keepdims=True)
    before_doc = jnp.sum(jnp.where(diagonal, before, 0), axis=1, keepdims=True)
    own_seen = (key_doc == own_docs) & (row <= column)
    own_bias[...] = jnp.where(own_seen, 0.0, HIDDEN)
    cross_bias[...] = jnp.where(own_seen | (before_doc == own_docs), 0.0, HIDDEN)
    crossing[...] = jnp.where(key_doc == before[:, length - 1 :], jnp.ones((length, length), jnp.float32), 0.0).astype(
        jnp.bfloat16
    )
    crossing_rows = jnp.sum(jnp.where(own_docs == before[:, length - 1 :], 1, 0))
    rows[0] = (crossing_rows + (ROW_TILE - 1)) // ROW_TILE * ROW_TILE
    for copy in copies:
        copy.wait()
    for g in range(KV):
        keys = key[:, head_columns(g)]
        values = value[:, head_columns(g)].T
        for head in range(g * PER_KV, (g + 1) * PER_KV, 2):
            weights, share = column_softmax(raw_scores(keys, query, head, own_bias[...]))
            mixed = jnp.dot(values, weights.astype(jnp.bfloat16), preferred_element_type=jnp.float32)
            mixed = (mixed * share).astype(jnp.bfloat16)
            own[:, head_columns(head)] = mixed[:, :length].T
            own[:, head_columns(head + 1)] = mixed[:, length:].T
        group = head_columns(g * PER_KV, PER_KV)
        pltpu.make_async_copy(own.at[:, group], out.at[:, group], out_sem).start()
    pltpu.make_async_copy(own, out, out_sem).wait()


def weight_kernel(
    query, key, key_near, key_far, value, value_near, cross_bias, crossing, weights_out, share_out, base, from_far, *, cuts
):
    length = key.shape[0]
    from_near = after_cut(cuts)
    mine = crossing[...] > 0
    from_far[...] = jnp.where(from_near, jnp.zeros_like(crossing), 1 - crossing[...])
    for g in range(KV):
        columns = head_columns(g)
        base[:, columns] = jnp.where(mine, value[:, columns], value_near[:, columns])
        behind = jnp.where(from_near, key_near[:, columns], key_far[:, columns])
        keys = jnp.where(mine, key[:, columns], behind)
        for head in range(g * PER_KV, (g + 1) * PER_KV, 2):
            weights, share = column_softmax(raw_scores(keys, query, head, cross_bias[...]))
            weights = weights.astype(jnp.bfloat16)
            for i in range(2):
                part = slice(i * length, (i + 1) * length)
                weights_out[head + i] = weights[:, part].T
                share_out[head + i] = jnp.broadcast_to(share[:, part], (HEAD, length)).T


def merge_kernel(weights, share, base, value_far, from_far, crossing, own, rows, early, out, held, sem):
    length = own.shape[0]
    far = from_far[...] > 0
    stored = jnp.maximum(rows[0], ROW_TILE)
    part = pl.ds(0, pl.multiple_of(stored, ROW_TILE))

    def merge_rows(count, together):
        mine = crossing[:count] > 0
        for g in range(KV):
            columns = head_columns(g)
            values = jnp.where(far, value_far[:, columns], base[:, columns])
            for head in range(g * PER_KV, (g + 1) * PER_KV, together):
                several = jnp.concatenate([weights[head + i, :count] for i in range(together)], axis=0)
                mixed = jnp.dot(several, values, preferred_element_type=jnp.float32)
                for i in range(together):
                    fresh = (mixed[i * count : (i + 1) * count] * share[head + i, :count]).astype(jnp.bfloat16)
                    held[:count, head_columns(head + i)] = jnp.where(mine, fresh, own[:count, head_columns(head + i)])
            group = head_columns(g * PER_KV, PER_KV)
            pltpu.make_async_copy(held.at[part, group], out.at[part, group], sem).start()

    half, most = length // 2, length * 3 // 4
    pl.when(stored > most)(lambda: merge_rows(length, PER_KV // 2))
    pl.when((stored > half) & (stored <= most))(lambda: merge_rows(most, PER_KV // 2))
    pl.when(stored <= half)(lambda: merge_rows(half, PER_KV))
    pltpu.make_async_copy(held.at[part], out.at[part], sem).wait()


def in_vmem(array):
    return pltpu.with_memory_space_constraint(array, pltpu.VMEM)


def one_block_back(queries, keys, values, doc_ids):
    count = lax.axis_size(TOKENS_AXES)
    length = queries.shape[0]
    cuts = cuts_of(count)
    rings, swap = rings_between(count, cuts), swapped(count)
    key_near = lax.ppermute(keys, TOKENS_AXES, swap)
    key_far = lax.ppermute(keys, TOKENS_AXES, rings)
    value_near = lax.ppermute(values, TOKENS_AXES, swap)
    value_far = lax.ppermute(values, TOKENS_AXES, rings)
    docs = doc_ids.reshape(-1, length)
    whole = pl.BlockSpec(memory_space=pltpu.VMEM)
    anywhere = pl.BlockSpec(memory_space=pl.ANY)
    hbm = pl.BlockSpec(memory_space=pltpu.HBM)
    scalars = pl.BlockSpec(memory_space=pltpu.SMEM)
    params = pltpu.CompilerParams(vmem_limit_bytes=KERNEL_VMEM)
    square = (length, length)
    own, query_held, key_held, value_held, cross_bias, crossing, rows, early = pl.pallas_call(
        own_kernel,
        out_shape=(
            pltpu.VMEM(queries.shape, jnp.bfloat16),
            pltpu.VMEM(queries.shape, jnp.bfloat16),
            pltpu.VMEM(keys.shape, jnp.bfloat16),
            pltpu.VMEM(values.shape, jnp.bfloat16),
            pltpu.VMEM(square, jnp.float32),
            pltpu.VMEM(square, jnp.bfloat16),
            pltpu.SMEM((1,), jnp.int32),
            pltpu.HBM(queries.shape, jnp.bfloat16),
        ),
        in_specs=[hbm] * 4,
        out_specs=[whole] * 6 + [scalars, hbm],
        scratch_shapes=[
            pltpu.VMEM(square, jnp.float32),
            pltpu.VMEM(docs.shape, jnp.int32),
            *[pltpu.SemaphoreType.DMA] * 5,
        ],
        compiler_params=params,
        name="own_attention",
    )(*(pltpu.with_memory_space_constraint(array, pltpu.HBM) for array in (queries, keys, values, docs)))
    weights, share, base, from_far = pl.pallas_call(
        functools.partial(weight_kernel, cuts=cuts),
        out_shape=(
            pltpu.VMEM((HQ,) + square, jnp.bfloat16),
            pltpu.VMEM((HQ,) + square, jnp.float32),
            pltpu.VMEM(values.shape, jnp.bfloat16),
            pltpu.VMEM(square, jnp.bfloat16),
        ),
        in_specs=[whole] * 8,
        out_specs=[whole] * 4,
        compiler_params=params,
        name="crossing_weights",
    )(
        query_held,
        key_held,
        in_vmem(key_near),
        in_vmem(key_far),
        value_held,
        in_vmem(value_near),
        cross_bias,
        crossing,
    )
    return pl.pallas_call(
        merge_kernel,
        out_shape=jax.ShapeDtypeStruct(queries.shape, jnp.bfloat16),
        in_specs=[whole] * 7 + [scalars, hbm],
        out_specs=hbm,
        scratch_shapes=[pltpu.VMEM(queries.shape, jnp.bfloat16), pltpu.SemaphoreType.DMA],
        input_output_aliases={8: 0},
        compiler_params=params,
        name="merge",
    )(weights, share, base, in_vmem(value_far), from_far, crossing, own, rows, early)


def blocks_back(queries, keys, values, doc_ids, blocks):
    count = lax.axis_size(TOKENS_AXES)
    length = queries.shape[0]
    me = lax.axis_index(TOKENS_AXES)
    halo = [
        (lax.ppermute(keys, TOKENS_AXES, ring(count, s)), lax.ppermute(values, TOKENS_AXES, ring(count, s)))
        for s in range(blocks, 0, -1)
    ] + [(keys, values)]
    window = (blocks + 1) * length
    key_all = jnp.concatenate([k for k, _ in halo], axis=0).reshape(window, KV, HEAD).transpose(1, 0, 2)
    value_all = jnp.concatenate([v for _, v in halo], axis=0).reshape(window, KV, HEAD).transpose(1, 0, 2)
    padded = jnp.concatenate([jnp.full((blocks * length,), -1, jnp.int32), doc_ids], axis=0)
    key_doc = lax.dynamic_slice_in_dim(padded, me * length, window, 0)
    query_doc = key_doc[blocks * length :]
    offset = jnp.arange(window, dtype=jnp.int32) - blocks * length
    visible = (key_doc[None, :] == query_doc[:, None]) & (offset[None, :] <= jnp.arange(length)[:, None])
    grouped = queries.reshape(length, KV, PER_KV, HEAD).transpose(1, 2, 0, 3)

    def one_head(operands):
        rows, key_rows, value_rows = operands
        raw = jnp.einsum("gqd,kd->gqk", rows, key_rows, preferred_element_type=jnp.float32)
        raw = jnp.where(visible[None], raw, HIDDEN)
        peak = jnp.max(raw, axis=-1, keepdims=True)
        weights = jnp.exp2((raw - peak) * EXPONENT)
        totals = jnp.sum(weights, axis=-1, keepdims=True)
        mixed = jnp.einsum("gqk,kd->gqd", weights.astype(jnp.bfloat16), value_rows, preferred_element_type=jnp.float32)
        return (mixed / totals).astype(jnp.bfloat16)

    mixed = lax.map(one_head, (grouped, key_all, value_all))
    return mixed.transpose(2, 0, 1, 3).reshape(length, HQ * HEAD)


def shards(queries, keys, values, doc_ids):
    length = queries.shape[0]
    reach = lax.axis_size("ulysses") * length // 4
    blocks = -(-reach // length)
    if blocks == 1 and length == HEAD:
        return one_block_back(queries, keys, values, doc_ids)
    return blocks_back(queries, keys, values, doc_ids, blocks)


def solution(mesh):
    placed = P(TOKENS_AXES, None)
    return jax.shard_map(
        shards, mesh=mesh, in_specs=(placed, placed, placed, P()), out_specs=placed, check_vma=False
    )
```

```python
import functools
import math

import jax
import jax.numpy as jnp
from jax import lax
from jax.experimental import pallas as pl
from jax.experimental.pallas import tpu as pltpu
from jax.sharding import PartitionSpec as P

HQ = 48
KV = 8
HEAD = 128
PER_KV = HQ // KV
TOKENS_AXES = ("ctx", "ulysses")
HIDDEN = -1e30
EXPONENT = math.log2(math.e) / math.sqrt(HEAD)
ROW_TILE = 32
KERNEL_VMEM = 16 * 1024 * 1024


def cuts_of(count):
    return [cut for cut in [4, 6] + list(range(14, count, 8)) if cut < count - 2]


def rings_between(count, cuts):
    pairs, first = [], 0
    for last in cuts + [count - 1]:
        pairs += [(i, i + 1) for i in range(first, last)] + [(last, first)]
        first = last + 1
    return pairs


def after_cut(cuts):
    me = lax.axis_index(TOKENS_AXES)
    return functools.reduce(jnp.logical_or, [me == cut + 1 for cut in cuts], False)


def ring(count, steps):
    return [(i, (i + steps) % count) for i in range(count)]


def swapped(count):
    return [(i, i ^ 1) for i in range(count)]


def head_columns(head, heads=1):
    return slice(head * HEAD, (head + heads) * HEAD)


def column_softmax(raw):
    peak = jnp.max(raw, axis=0, keepdims=True)
    weights = jnp.exp2((raw - peak) * EXPONENT)
    return weights, 1.0 / jnp.sum(weights, axis=0, keepdims=True)


def raw_scores(keys, query, head, bias):
    raw = lax.dot_general(
        keys,
        jnp.concatenate([query[:, head_columns(head)], query[:, head_columns(head + 1)]], axis=0),
        (((1,), (1,)), ((), ())),
        preferred_element_type=jnp.float32,
    )
    return raw + jnp.concatenate([bias, bias], axis=1)


def own_kernel(
    query_in,
    key_in,
    value_in,
    docs_in,
    own,
    query,
    key,
    value,
    cross_bias,
    crossing,
    rows,
    out,
    own_bias,
    docs,
    docs_sem,
    key_sem,
    value_sem,
    query_sem,
    out_sem,
):
    length = key.shape[0]
    docs_copy = pltpu.make_async_copy(docs_in, docs, docs_sem)
    pieces = [(key_in, key, key_sem), (value_in, value, value_sem), (query_in, query, query_sem)]
    copies = [pltpu.make_async_copy(source, target, sem) for source, target, sem in pieces]
    docs_copy.start()
    for copy in copies:
        copy.start()
    docs_copy.wait()
    me = lax.axis_index(TOKENS_AXES)
    own_docs = docs[pl.ds(me, 1), :]
    before = jnp.where(me > 0, docs[pl.ds(jnp.maximum(me - 1, 0), 1), :], -1)
    row = lax.broadcasted_iota(jnp.int32, (length, length), 0)
    column = lax.broadcasted_iota(jnp.int32, (length, length), 1)
    diagonal = row == column
    key_doc = jnp.sum(jnp.where(diagonal, own_docs, 0), axis=1, keepdims=True)
    before_doc = jnp.sum(jnp.where(diagonal, before, 0), axis=1, keepdims=True)
    own_seen = (key_doc == own_docs) & (row <= column)
    own_bias[...] = jnp.where(own_seen, 0.0, HIDDEN)
    cross_bias[...] = jnp.where(own_seen | (before_doc == own_docs), 0.0, HIDDEN)
    crossing[...] = jnp.where(key_doc == before[:, length - 1 :], jnp.ones((length, length), jnp.float32), 0.0).astype(
        jnp.bfloat16
    )
    crossing_rows = jnp.sum(jnp.where(own_docs == before[:, length - 1 :], 1, 0))
    rows[0] = (crossing_rows + (ROW_TILE - 1)) // ROW_TILE * ROW_TILE
    for copy in copies:
        copy.wait()
    for g in range(KV):
        keys = key[:, head_columns(g)]
        values = value[:, head_columns(g)].T
        for head in range(g * PER_KV, (g + 1) * PER_KV, 2):
            weights, share = column_softmax(raw_scores(keys, query, head, own_bias[...]))
            mixed = jnp.dot(values, weights.astype(jnp.bfloat16), preferred_element_type=jnp.float32)
            mixed = (mixed * share).astype(jnp.bfloat16)
            own[:, head_columns(head)] = mixed[:, :length].T
            own[:, head_columns(head + 1)] = mixed[:, length:].T
        group = head_columns(g * PER_KV, PER_KV)
        pltpu.make_async_copy(own.at[:, group], out.at[:, group], out_sem).start()
    pltpu.make_async_copy(own, out, out_sem).wait()


def weight_kernel(
    query, key, key_near, key_far, value, value_near, cross_bias, crossing, weights_out, share_out, base, from_far, *, cuts
):
    length = key.shape[0]
    from_near = after_cut(cuts)
    mine = crossing[...] > 0
    from_far[...] = jnp.where(from_near, jnp.zeros_like(crossing), 1 - crossing[...])
    for g in range(KV):
        columns = head_columns(g)
        base[:, columns] = jnp.where(mine, value[:, columns], value_near[:, columns])
        behind = jnp.where(from_near, key_near[:, columns], key_far[:, columns])
        keys = jnp.where(mine, key[:, columns], behind)
        for head in range(g * PER_KV, (g + 1) * PER_KV, 2):
            weights, share = column_softmax(raw_scores(keys, query, head, cross_bias[...]))
            weights = weights.astype(jnp.bfloat16)
            for i in range(2):
                part = slice(i * length, (i + 1) * length)
                weights_out[head + i] = weights[:, part].T
                share_out[head + i] = jnp.broadcast_to(share[:, part], (HEAD, length)).T


def merge_kernel(weights, share, base, value_far, from_far, crossing, own, rows, early, out, held, sem):
    length = own.shape[0]
    far = from_far[...] > 0
    stored = jnp.maximum(rows[0], ROW_TILE)
    part = pl.ds(0, pl.multiple_of(stored, ROW_TILE))

    def merge_rows(count, together):
        mine = crossing[:count] > 0
        for g in range(KV):
            columns = head_columns(g)
            values = jnp.where(far, value_far[:, columns], base[:, columns])
            for head in range(g * PER_KV, (g + 1) * PER_KV, together):
                several = jnp.concatenate([weights[head + i, :count] for i in range(together)], axis=0)
                mixed = jnp.dot(several, values, preferred_element_type=jnp.float32)
                for i in range(together):
                    fresh = (mixed[i * count : (i + 1) * count] * share[head + i, :count]).astype(jnp.bfloat16)
                    held[:count, head_columns(head + i)] = jnp.where(mine, fresh, own[:count, head_columns(head + i)])
            group = head_columns(g * PER_KV, PER_KV)
            pltpu.make_async_copy(held.at[part, group], out.at[part, group], sem).start()

    pl.when(stored <= length // 2)(lambda: merge_rows(length // 2, PER_KV))
    pl.when(stored > length // 2)(lambda: merge_rows(length, PER_KV // 2))
    pltpu.make_async_copy(held.at[part], out.at[part], sem).wait()


def in_vmem(array):
    return pltpu.with_memory_space_constraint(array, pltpu.VMEM)


def one_block_back(queries, keys, values, doc_ids):
    count = lax.axis_size(TOKENS_AXES)
    length = queries.shape[0]
    cuts = cuts_of(count)
    rings, swap = rings_between(count, cuts), swapped(count)
    key_near = lax.ppermute(keys, TOKENS_AXES, swap)
    key_far = lax.ppermute(keys, TOKENS_AXES, rings)
    value_near = lax.ppermute(values, TOKENS_AXES, swap)
    value_far = lax.ppermute(values, TOKENS_AXES, rings)
    docs = doc_ids.reshape(-1, length)
    whole = pl.BlockSpec(memory_space=pltpu.VMEM)
    anywhere = pl.BlockSpec(memory_space=pl.ANY)
    hbm = pl.BlockSpec(memory_space=pltpu.HBM)
    scalars = pl.BlockSpec(memory_space=pltpu.SMEM)
    params = pltpu.CompilerParams(vmem_limit_bytes=KERNEL_VMEM)
    square = (length, length)
    own, query_held, key_held, value_held, cross_bias, crossing, rows, early = pl.pallas_call(
        own_kernel,
        out_shape=(
            pltpu.VMEM(queries.shape, jnp.bfloat16),
            pltpu.VMEM(queries.shape, jnp.bfloat16),
            pltpu.VMEM(keys.shape, jnp.bfloat16),
            pltpu.VMEM(values.shape, jnp.bfloat16),
            pltpu.VMEM(square, jnp.float32),
            pltpu.VMEM(square, jnp.bfloat16),
            pltpu.SMEM((1,), jnp.int32),
            pltpu.HBM(queries.shape, jnp.bfloat16),
        ),
        in_specs=[hbm] * 4,
        out_specs=[whole] * 6 + [scalars, hbm],
        scratch_shapes=[
            pltpu.VMEM(square, jnp.float32),
            pltpu.VMEM(docs.shape, jnp.int32),
            *[pltpu.SemaphoreType.DMA] * 5,
        ],
        compiler_params=params,
        name="own_attention",
    )(*(pltpu.with_memory_space_constraint(array, pltpu.HBM) for array in (queries, keys, values, docs)))
    weights, share, base, from_far = pl.pallas_call(
        functools.partial(weight_kernel, cuts=cuts),
        out_shape=(
            pltpu.VMEM((HQ,) + square, jnp.bfloat16),
            pltpu.VMEM((HQ,) + square, jnp.float32),
            pltpu.VMEM(values.shape, jnp.bfloat16),
            pltpu.VMEM(square, jnp.bfloat16),
        ),
        in_specs=[whole] * 8,
        out_specs=[whole] * 4,
        compiler_params=params,
        name="crossing_weights",
    )(
        query_held,
        key_held,
        in_vmem(key_near),
        in_vmem(key_far),
        value_held,
        in_vmem(value_near),
        cross_bias,
        crossing,
    )
    return pl.pallas_call(
        merge_kernel,
        out_shape=jax.ShapeDtypeStruct(queries.shape, jnp.bfloat16),
        in_specs=[whole] * 7 + [scalars, hbm],
        out_specs=hbm,
        scratch_shapes=[pltpu.VMEM(queries.shape, jnp.bfloat16), pltpu.SemaphoreType.DMA],
        input_output_aliases={8: 0},
        compiler_params=params,
        name="merge",
    )(weights, share, base, in_vmem(value_far), from_far, crossing, own, rows, early)


def blocks_back(queries, keys, values, doc_ids, blocks):
    count = lax.axis_size(TOKENS_AXES)
    length = queries.shape[0]
    me = lax.axis_index(TOKENS_AXES)
    halo = [
        (lax.ppermute(keys, TOKENS_AXES, ring(count, s)), lax.ppermute(values, TOKENS_AXES, ring(count, s)))
        for s in range(blocks, 0, -1)
    ] + [(keys, values)]
    window = (blocks + 1) * length
    key_all = jnp.concatenate([k for k, _ in halo], axis=0).reshape(window, KV, HEAD).transpose(1, 0, 2)
    value_all = jnp.concatenate([v for _, v in halo], axis=0).reshape(window, KV, HEAD).transpose(1, 0, 2)
    padded = jnp.concatenate([jnp.full((blocks * length,), -1, jnp.int32), doc_ids], axis=0)
    key_doc = lax.dynamic_slice_in_dim(padded, me * length, window, 0)
    query_doc = key_doc[blocks * length :]
    offset = jnp.arange(window, dtype=jnp.int32) - blocks * length
    visible = (key_doc[None, :] == query_doc[:, None]) & (offset[None, :] <= jnp.arange(length)[:, None])
    grouped = queries.reshape(length, KV, PER_KV, HEAD).transpose(1, 2, 0, 3)

    def one_head(operands):
        rows, key_rows, value_rows = operands
        raw = jnp.einsum("gqd,kd->gqk", rows, key_rows, preferred_element_type=jnp.float32)
        raw = jnp.where(visible[None], raw, HIDDEN)
        peak = jnp.max(raw, axis=-1, keepdims=True)
        weights = jnp.exp2((raw - peak) * EXPONENT)
        totals = jnp.sum(weights, axis=-1, keepdims=True)
        mixed = jnp.einsum("gqk,kd->gqd", weights.astype(jnp.bfloat16), value_rows, preferred_element_type=jnp.float32)
        return (mixed / totals).astype(jnp.bfloat16)

    mixed = lax.map(one_head, (grouped, key_all, value_all))
    return mixed.transpose(2, 0, 1, 3).reshape(length, HQ * HEAD)


def shards(queries, keys, values, doc_ids):
    length = queries.shape[0]
    reach = lax.axis_size("ulysses") * length // 4
    blocks = -(-reach // length)
    if blocks == 1 and length == HEAD:
        return one_block_back(queries, keys, values, doc_ids)
    return blocks_back(queries, keys, values, doc_ids, blocks)


def solution(mesh):
    placed = P(TOKENS_AXES, None)
    return jax.shard_map(
        shards, mesh=mesh, in_specs=(placed, placed, placed, P()), out_specs=placed, check_vma=False
    )
```
